32 devices in a mesh: seq: 2 (over x), head: 4 (over y, core), dp: 4 (over z).
Axes of the slice: x: 2, y: 2, z: 4, core: 2. Of those that a mesh axis runs over, the one named last changes fastest.
Arguments:
- layer_input: bfloat16 [4, 256, 4096], P('dp', 'seq', 'head'), may hold values from -24 to 24
- head_input: bfloat16 [4, 256, 4096], P('dp', 'seq', 'head'), may hold values from -6 to 6
- in_matrix: bfloat16 [4, 256, 512], P('dp', 'seq', 'head'), may hold values from -6 to 6
- out_matrix: bfloat16 [4, 256, 512], P('dp', 'seq', 'head'), may hold values from -6 to 6
- grad_output: bfloat16 [4, 256, 4096], P('dp', 'seq', 'head'), may hold values from -0.59765625 to 0.59765625
- step_weight: bfloat16 [4096, 64], P(None, 'head'), may hold values from -0.09375 to 0.09375
- step_bias: float32 [64], P('head'), may hold values from -7 to -6
- decay_log: float32 [64], P('head'), may hold values from -6.22 to 2.78
Outputs:
- grad_heads: bfloat16 [4, 256, 4096], P('dp', 'seq', 'head')
- grad_in_matrix: bfloat16 [4, 256, 512], P('dp', 'seq', 'head')
- grad_out_matrix: bfloat16 [4, 256, 512], P('dp', 'seq', 'head')
- grad_layer_input: bfloat16 [4, 256, 4096], P('dp', 'seq', 'head')
- grad_step_weight: float32 [4096, 64], P(('seq', 'dp'), 'head')
The draws below stay inside these ranges and needn't reach their ends.
All inputs are finite; a program needn't handle non-finite values.
Results may differ from the reference program's by a relative error of at most 0.02.
Values may be sent and summed in bfloat16 or wider, within the bound.
A program may use at most 64 MiB of HBM per device.

```python
import math
import jax
import jax.numpy as jnp
from jax import lax

D = 4096
H = 64
P_SIZE = 64
NSTATE = 128
G = 4
BLOCK = 128
TOK_DEV = 128
BATCH = 4
LEN = 256
N_HEAD = 4


def draw_layer_input(key, part):
    first_key, second_key, third_key = jax.random.split(key, 3)
    base = jnp.clip(jax.random.normal(first_key, (BATCH, LEN, D), jnp.float32), -5.0, 5.0)
    block_count = LEN // TOK_DEV
    scales = jnp.exp(jax.random.uniform(second_key, (BATCH, block_count), jnp.float32, math.log(0.6), math.log(1.6)))
    row_scale = jnp.repeat(scales, TOK_DEV, axis=1)
    spots = jax.random.randint(third_key, (BATCH, 6), 0, LEN)
    positions = jnp.arange(LEN)
    struck = jnp.any(positions[None, :, None] == spots[:, None, :], axis=2)
    factor = jnp.where(struck, 3.0, 1.0)
    return (base * (row_scale * factor)[..., None]).astype(jnp.bfloat16)


def draw_decay_log(key, part):
    values = jax.random.uniform(key, (H,), jnp.float32, math.log(0.002), math.log(16.0))
    return values.astype(jnp.float32)


def block_levels(key, extent, cuts, low, high):
    def one(axis_at, parts):
        heights = jax.random.uniform(jax.random.fold_in(jax.random.fold_in(key, 6), axis_at), (parts,), jnp.float32, low / len(cuts), high / len(cuts))
        return jnp.repeat(jnp.exp(heights), extent[axis_at] // parts).reshape((-1,) + (1,) * (len(extent) - axis_at - 1))

    loudness = one(*cuts[0])
    for cut in cuts[1:]:
        loudness = loudness * one(*cut)
    return loudness


def bell_draw(own_key, shape, spread, reach, pieces=(), held_as=jnp.bfloat16):
    array = spread * jax.random.normal(own_key, shape, jnp.float32)
    if pieces:
        array = array * block_levels(own_key, shape, pieces, -0.22, 0.18)
    return jnp.clip(array, -reach, reach).astype(held_as)


def setup_inputs(seed: int = 0) -> dict:
    seeds = jax.random.split(jax.random.key(seed), 9)
    layer_input = draw_layer_input(jax.random.fold_in(seeds[8], 71), 0)
    head_input = bell_draw(seeds[1], (BATCH, LEN, H * P_SIZE), 1.0, 6.0, ((0, 4), (1, 2), (2, 4)))
    in_matrix = bell_draw(seeds[2], (BATCH, LEN, G * NSTATE), 1.0, 6.0, ((0, 4), (1, 2), (2, 4)))
    out_matrix = bell_draw(seeds[3], (BATCH, LEN, G * NSTATE), 1.0, 6.0, ((0, 4), (1, 2), (2, 4)))
    grad_output = bell_draw(seeds[4], (BATCH, LEN, H * P_SIZE), 0.1, 0.59765625, ((0, 4), (1, 2), (2, 4)))
    step_weight = bell_draw(seeds[5], (D, H), D ** -0.5, 0.09375, ((1, 4),))
    step_bias = jnp.clip(-7.0 + 1.0 * jax.random.uniform(seeds[6], (H,), jnp.float32) ** block_levels(seeds[6], (H,), ((0, 4),), -0.2, 0.2), -7.0, -6.0)
    decay_log = draw_decay_log(jax.random.fold_in(seeds[8], 71), 0)
    return {"layer_input": layer_input, "head_input": head_input, "in_matrix": in_matrix, "out_matrix": out_matrix, "grad_output": grad_output, "step_weight": step_weight, "step_bias": step_bias, "decay_log": decay_log}


PRECISION_LEVEL = lax.Precision.HIGHEST

def block_step(carry_state, inputs):
    input_block, b_block, c_block, step_block, decay_block = inputs
    cumulated = jnp.cumsum(decay_block, axis=-1)
    block_len = cumulated.shape[-1]
    lower_mask = jnp.arange(block_len)[:, None] >= jnp.arange(block_len)[None, :]
    decay_span = jnp.exp(jnp.where(lower_mask, cumulated[..., :, None] - cumulated[..., None, :], -1e+30))
    kernel = jnp.einsum('tgn,sgn->gts', c_block, b_block, precision=PRECISION_LEVEL)
    weight_values = kernel[:, None] * decay_span * step_block[..., None, :]
    within_block = jnp.einsum('idwz,zidx->widx', weight_values, input_block, precision=PRECISION_LEVEL)
    carried = jnp.einsum('tgn,grnp->tgrp', c_block, carry_state, precision=PRECISION_LEVEL)
    output = within_block + jnp.moveaxis(jnp.exp(cumulated), -1, 0)[..., None] * carried
    totals = cumulated[..., -1]
    inflow = jnp.exp(totals[..., None] - cumulated) * step_block
    fresh_term = jnp.einsum('grs,sgn,sgrp->grnp', inflow, b_block, input_block, precision=PRECISION_LEVEL)
    return (jnp.exp(totals)[..., None, None] * carry_state + fresh_term, output)

def segment(x_rows, b_rows, readout_rows, step_sizes, decays, start_state):
    length = x_rows.shape[0]
    blocks = length // BLOCK

    def split_rows(values):
        return values.reshape((blocks, BLOCK) + values.shape[1:])

    def split_last(values):
        return jnp.moveaxis(values.reshape(values.shape[:-1] + (blocks, BLOCK)), -2, 0)
    final_state, outputs = lax.scan(block_step, start_state, (split_rows(x_rows), split_rows(b_rows), split_rows(readout_rows), split_last(step_sizes), split_last(decays)))
    return (outputs.reshape(x_rows.shape), final_state)

def reference(layer_input, head_input, in_matrix, out_matrix, grad_output, step_weight, step_bias, decay_log):
    ratio = H // G
    rates = jnp.exp(decay_log).reshape(G, ratio)
    heads_per_shard = H // N_HEAD

    def one_sequence(items):
        seq_input, seq_heads, seq_in, seq_out, seq_grad = items
        preact = jnp.dot(seq_input, step_weight, preferred_element_type=jnp.float32) + step_bias
        step_sizes = jnp.transpose(jax.nn.softplus(preact)).reshape(G, ratio, LEN)
        x_rows = seq_heads.astype(jnp.float32).reshape(LEN, G, ratio, P_SIZE)
        b_rows = seq_in.astype(jnp.float32).reshape(LEN, G, NSTATE)
        readout_rows = seq_out.astype(jnp.float32).reshape(LEN, G, NSTATE)
        output_gradient = seq_grad.astype(jnp.float32).reshape(LEN, G, ratio, P_SIZE)
        start_state = jnp.zeros((G, ratio, NSTATE, P_SIZE), jnp.float32)

        def forward(x_arg, b_arg, c_arg, step_arg):
            return segment(x_arg, b_arg, c_arg, step_arg, -rates[..., None] * step_arg, start_state)[0]
        forward_out, pullback = jax.vjp(forward, x_rows, b_rows, readout_rows, step_sizes)
        grad_x, grad_b, grad_c, grad_step = pullback(output_gradient)
        grad_pre = (jnp.transpose(grad_step.reshape(H, LEN)) * jax.nn.sigmoid(preact)).astype(jnp.bfloat16)
        grad_input = jnp.zeros((LEN, D), jnp.float32)
        for shard_index in range(N_HEAD):
            first = shard_index * heads_per_shard
            partial_value = lax.dot_general(grad_pre[:, first:first + heads_per_shard], step_weight[:, first:first + heads_per_shard], (((1,), (1,)), ((), ())), preferred_element_type=jnp.float32)
            grad_input = grad_input + lax.optimization_barrier(partial_value.astype(jnp.bfloat16)).astype(jnp.float32)
        grad_weight = lax.dot_general(seq_input, grad_pre, (((0,), (0,)), ((), ())), preferred_element_type=jnp.float32)
        return (grad_x.reshape(LEN, H * P_SIZE).astype(jnp.bfloat16), grad_b.reshape(LEN, G * NSTATE).astype(jnp.bfloat16), grad_c.reshape(LEN, G * NSTATE).astype(jnp.bfloat16), grad_input.astype(jnp.bfloat16), grad_weight)
    results = lax.map(one_sequence, (layer_input, head_input, in_matrix, out_matrix, grad_output))
    return (results[0], results[1], results[2], results[3], lax.optimization_barrier(jnp.sum(results[4], axis=0)))
```

```python
import functools

import jax
import jax.numpy as jnp
from jax import lax
from jax.experimental import pallas as pl
from jax.experimental.pallas import tpu as pltpu
from jax.sharding import PartitionSpec as P

H = 64
P_SIZE = 64
NSTATE = 128
G = 4
BLOCK = 128


PRECISION_LEVEL = lax.Precision.HIGHEST


def prefix(value, axis, join, neutral, backward):
    count = lax.axis_size(axis)
    place = lax.axis_index(axis)
    ahead = count - 1 - place if backward else place
    gathered = jax.tree.map(
        lambda a, kind: lax.all_gather(a.astype(kind), axis), value, (jnp.bfloat16, jnp.bfloat16)
    )
    state = jax.tree.map(lambda a, e: jnp.zeros_like(a) + jnp.asarray(e, a.dtype), value, neutral)

    def one(step, state):
        source = count - 1 - step if backward else step
        return join(
            state,
            jax.tree.map(
                lambda a, own: lax.dynamic_index_in_dim(a, source, 0, False).astype(own.dtype),
                gathered,
                value,
            ),
        )

    return lax.fori_loop(0, ahead, one, state)


def block_step(carry_state, inputs):
    input_block, b_block, c_block, step_block, decay_block = inputs
    cumulated = jnp.cumsum(decay_block, axis=-1)
    block_len = cumulated.shape[-1]
    lower_mask = jnp.arange(block_len)[:, None] >= jnp.arange(block_len)[None, :]
    decay_span = jnp.exp(
        jnp.where(lower_mask, cumulated[..., :, None] - cumulated[..., None, :], -1e30)
    )
    kernel = jnp.einsum("tgn,sgn->gts", c_block, b_block, precision=PRECISION_LEVEL)
    weight_values = kernel[:, None] * decay_span * step_block[..., None, :]
    within_block = jnp.einsum(
        "idwz,zidx->widx", weight_values, input_block, precision=PRECISION_LEVEL
    )
    carried = jnp.einsum("tgn,grnp->tgrp", c_block, carry_state, precision=PRECISION_LEVEL)
    output = within_block + jnp.moveaxis(jnp.exp(cumulated), -1, 0)[..., None] * carried
    totals = cumulated[..., -1]
    inflow = jnp.exp(totals[..., None] - cumulated) * step_block
    fresh_term = jnp.einsum(
        "grs,sgn,sgrp->grnp", inflow, b_block, input_block, precision=PRECISION_LEVEL
    )
    return (jnp.exp(totals)[..., None, None] * carry_state + fresh_term, output)


def segment(x_rows, b_rows, readout_rows, step_sizes, decays, start_state):
    length = x_rows.shape[0]
    blocks = length // BLOCK

    def split_rows(values):
        return values.reshape((blocks, BLOCK) + values.shape[1:])

    def split_last(values):
        return jnp.moveaxis(values.reshape(values.shape[:-1] + (blocks, BLOCK)), -2, 0)

    final_state, outputs = lax.scan(
        block_step,
        start_state,
        (
            split_rows(x_rows),
            split_rows(b_rows),
            split_rows(readout_rows),
            split_last(step_sizes),
            split_last(decays),
        ),
    )
    return (outputs.reshape(x_rows.shape), final_state)


def join_pairs(earlier, later):
    return (earlier[0] + later[0], jnp.exp(later[0])[..., None, None] * earlier[1] + later[1])


def body(
    layer_input, head_input, in_matrix, out_matrix, grad_output, step_weight, step_bias, decay_log
):
    tokens = head_input.shape[1]
    group_count = in_matrix.shape[2] // NSTATE
    ratio = H // G
    heads_here = group_count * ratio
    whole_input = lax.all_gather(layer_input, "head", axis=2, tiled=True)[0]
    preact = jnp.dot(whole_input, step_weight, preferred_element_type=jnp.float32) + step_bias
    step_sizes = jnp.transpose(jax.nn.softplus(preact)).reshape(group_count, ratio, tokens)
    rates = jnp.exp(decay_log).reshape(group_count, ratio)
    decays = -rates[..., None] * step_sizes
    x_rows = head_input[0].astype(jnp.float32).reshape(tokens, group_count, ratio, P_SIZE)
    b_rows = in_matrix[0].astype(jnp.float32).reshape(tokens, group_count, NSTATE)
    readout_rows = out_matrix[0].astype(jnp.float32).reshape(tokens, group_count, NSTATE)
    output_gradient = grad_output[0].astype(jnp.float32).reshape(tokens, group_count, ratio, P_SIZE)
    running_state = jnp.cumsum(decays, axis=-1)
    totals = running_state[..., -1]
    local_state = jnp.einsum(
        "grs,sgn,sgrp->grnp",
        jnp.exp(totals[..., None] - running_state) * step_sizes,
        b_rows,
        x_rows,
        precision=PRECISION_LEVEL,
    )
    local_grad = jnp.einsum(
        "vad,dvm,dvah->vamh",
        jnp.exp(running_state),
        readout_rows,
        output_gradient,
        precision=PRECISION_LEVEL,
    )
    neutral = (jnp.zeros_like(totals), jnp.zeros_like(local_state))
    incoming = prefix((totals, local_state), "seq", join_pairs, neutral, False)[1]
    outgoing = prefix((totals, local_grad), "seq", join_pairs, neutral, True)[1]

    def local_map(x_arg, b_arg, c_arg, step_arg):
        return segment(x_arg, b_arg, c_arg, step_arg, -rates[..., None] * step_arg, incoming)

    forward_out, pullback = jax.vjp(local_map, x_rows, b_rows, readout_rows, step_sizes)
    grad_x, grad_b, grad_c, grad_step = pullback((output_gradient, outgoing))
    grad_pre = (
        jnp.transpose(grad_step.reshape(heads_here, tokens)) * jax.nn.sigmoid(preact)
    ).astype(jnp.bfloat16)
    partial_terms = lax.dot_general(
        grad_pre, step_weight, (((1,), (1,)), ((), ())), preferred_element_type=jnp.float32
    )
    grad_input = lax.psum_scatter(
        partial_terms.astype(jnp.bfloat16), "head", scatter_dimension=1, tiled=True
    )
    seq_part = lax.psum_scatter(
        lax.dot_general(
            whole_input, grad_pre, (((0,), (0,)), ((), ())), preferred_element_type=jnp.float32
        ).astype(jnp.bfloat16),
        "seq",
        scatter_dimension=0,
        tiled=True,
    ).astype(jnp.float32)
    grad_weight = lax.psum_scatter(seq_part, "dp", scatter_dimension=0, tiled=True)
    return (
        grad_x.reshape(tokens, heads_here * P_SIZE).astype(jnp.bfloat16)[None],
        grad_b.reshape(tokens, group_count * NSTATE).astype(jnp.bfloat16)[None],
        grad_c.reshape(tokens, group_count * NSTATE).astype(jnp.bfloat16)[None],
        grad_input[None],
        grad_weight,
    )


MESH = pl.DeviceIdType.MESH
NT = (((1,), (1,)), ((), ()))
NN = (((1,), (0,)), ((), ()))
TN = (((0,), (0,)), ((), ()))


def mm(a, b, dims):
    return lax.dot_general(a, b, dims, preferred_element_type=jnp.float32)


def exact_mm(a, b):
    return lax.dot_general(
        a, b, NN, precision=lax.Precision.HIGHEST, preferred_element_type=jnp.float32
    )


def two_parts(v):
    high = v.astype(jnp.bfloat16)
    low = (v - high.astype(jnp.float32)).astype(jnp.bfloat16)
    return high, low


def softplus(v):
    return jnp.maximum(v, 0.0) + jnp.log1p(jnp.exp(-jnp.abs(v)))


def mixer_kernel(
    sizes,
    layer_hbm, x_hbm, b_hbm, c_hbm, gy_hbm, w_hbm, bias_ref, rate_ref,
    gx_ref, gb_ref, gc_ref, gin_ref, gw_ref,
    layer, xg, bc, far_xg, far_bc, w_all, part, part_far, mt, ke, qcol, gp_all, gw_send, gw_recv,
    load_sem, w_send, w_recv, raw_send, raw_recv, p_send, p_recv, g_send, g_recv, d_send, d_recv,
):
    n_seq, n_head, n_dp, heads, p_size = sizes
    tokens, feats = layer.shape
    me_s, me_h, me_d = lax.axis_index("seq"), lax.axis_index("head"), lax.axis_index("dp")
    far_s = 1 - me_s
    rows_out = gw_ref.shape[1]
    cuts = feats // rows_out
    share = n_seq * n_dp

    def head_at(k):
        return lax.rem(me_h + k, n_head)

    def place(s, h, d):
        return {"seq": s, "head": h, "dp": d}

    loads = [
        pltpu.make_async_copy(x_hbm, xg.at[0], load_sem.at[0]),
        pltpu.make_async_copy(gy_hbm, xg.at[1], load_sem.at[1]),
        pltpu.make_async_copy(b_hbm, bc.at[0], load_sem.at[2]),
        pltpu.make_async_copy(c_hbm, bc.at[1], load_sem.at[3]),
        pltpu.make_async_copy(layer_hbm, layer, load_sem.at[4]),
        pltpu.make_async_copy(
            w_hbm.at[:, pl.ds(pl.multiple_of(me_h * feats, feats), feats)],
            w_all.at[pl.ds(pl.multiple_of(me_h * heads, heads), heads)],
            load_sem.at[5],
        ),
    ]
    for load in loads:
        load.start()

    barrier = pltpu.get_barrier_semaphore()
    my_row = me_s * n_dp + me_d
    source_h = my_row // cuts
    for k in range(n_head):
        if k:
            pl.semaphore_signal(
                barrier, inc=1, device_id=place(me_s, head_at(k), me_d), device_id_type=MESH
            )
        pl.semaphore_signal(
            barrier, inc=1, device_id=place(far_s, head_at(k), me_d), device_id_type=MESH
        )
    mine = source_h == me_h
    for k in range(share):
        spot = lax.rem(my_row + k, share)

        def greet():
            pl.semaphore_signal(
                barrier,
                inc=1,
                device_id=place(spot // n_dp, source_h, lax.rem(spot, n_dp)),
                device_id_type=MESH,
            )

        if k:
            greet()
        else:
            pl.when(jnp.logical_not(mine))(greet)
    pl.semaphore_wait(barrier, 2 * n_head - 1 + share - jnp.where(mine, 1, 0))

    w_copies = []
    for k in range(1, n_head):
        to = head_at(k)
        copy = pltpu.make_async_remote_copy(
            src_ref=w_hbm.at[:, pl.ds(pl.multiple_of(to * feats, feats), feats)],
            dst_ref=w_all.at[pl.ds(pl.multiple_of(me_h * heads, heads), heads)],
            send_sem=w_send.at[k - 1],
            recv_sem=w_recv.at[k - 1],
            device_id=place(me_s, to, me_d),
            device_id_type=MESH,
        )
        copy.start()
        w_copies.append(copy)

    for load in loads[:4]:
        load.wait()
    raw_copies = []
    for at, (near, far) in enumerate(((bc, far_bc), (xg, far_xg))):
        copy = pltpu.make_async_remote_copy(
            src_ref=near.at[me_s],
            dst_ref=far,
            send_sem=raw_send.at[at],
            recv_sem=raw_recv.at[at],
            device_id=place(far_s, me_h, me_d),
            device_id_type=MESH,
        )
        copy.start()
        raw_copies.append(copy)

    pair = 2 * p_size
    left = lax.broadcasted_iota(jnp.int32, (tokens, pair), 1) < p_size
    kt = mm(bc[0], bc[1], NT)
    zero_pair = jnp.zeros((tokens, pair), jnp.bfloat16)
    for j in range(heads // 2):
        lanes = slice(j * pair, (j + 1) * pair)
        x_pair, gy_pair = xg[0, :, lanes], xg[1, :, lanes]
        mt[2 * j] = mm(jnp.where(left, x_pair, zero_pair), gy_pair, NT)
        mt[2 * j + 1] = mm(jnp.where(left, zero_pair, x_pair), gy_pair, NT)

    loads[4].wait()
    loads[5].wait()
    for copy in w_copies:
        copy.wait_recv()
    part[...] = mm(w_all[...], layer[...], NT)
    part_copies = []
    for k in range(n_head):
        to = head_at(k)
        for hop in range(2):
            if k == 0 and hop == 0:
                continue
            at = 2 * k + hop - 1
            copy = pltpu.make_async_remote_copy(
                src_ref=part.at[pl.ds(pl.multiple_of(to * heads, heads), heads)],
                dst_ref=part_far.at[at],
                send_sem=p_send.at[at],
                recv_sem=p_recv.at[at],
                device_id=place(far_s if hop else me_s, to, me_d),
                device_id_type=MESH,
            )
            copy.start()
            part_copies.append(copy)

    upper = (
        lax.broadcasted_iota(jnp.int32, (tokens, tokens), 0)
        <= lax.broadcasted_iota(jnp.int32, (tokens, tokens), 1)
    )
    summing = upper.astype(jnp.float32)
    square = lax.broadcasted_iota(jnp.int32, (heads, heads), 0) == lax.broadcasted_iota(
        jnp.int32, (heads, heads), 1
    )

    def column(row):
        return jnp.sum(jnp.where(square, row, 0.0), axis=1, keepdims=True)

    bias = column(bias_ref[...])
    rate = jnp.exp(column(rate_ref[...]))
    spread_rows = lax.rem(lax.broadcasted_iota(jnp.int32, (2 * heads, heads * p_size), 0), heads)
    spread_at = lax.broadcasted_iota(jnp.int32, (2 * heads, heads * p_size), 1) // p_size
    spread = jnp.where(spread_rows == spread_at, 1.0, 0.0).astype(jnp.bfloat16)

    def widen(v):
        high, low = two_parts(v)
        return mm(jnp.concatenate([high, low], axis=0), spread, TN)

    for k in range(1, n_head):
        part_copies[2 * k - 1].wait_recv()
    preact = part[pl.ds(pl.multiple_of(me_h * heads, heads), heads), :] + bias
    for k in range(1, n_head):
        preact = preact + part_far[2 * k - 1]
    dt = softplus(preact)
    cum = exact_mm(-rate * dt, summing)
    total = cum[:, tokens - 1 :]
    cum_col = jnp.transpose(cum)
    dt_col = jnp.transpose(dt)
    dkt = jnp.zeros((tokens, tokens), jnp.float32)
    r_rows = []
    for h in range(heads):
        gap = cum[h : h + 1, :] - cum_col[:, h : h + 1]
        span = jnp.exp(jnp.where(upper, gap, -1e30))
        ke[h] = (kt * span).astype(jnp.bfloat16)
        step_here = dt_col[:, h : h + 1]
        f = mt[h] * span
        dkt = dkt + f * step_here
        prod = f * kt
        qcol[:, h : h + 1] = jnp.sum(prod, axis=1, keepdims=True)
        r_rows.append(jnp.sum(prod * step_here, axis=0, keepdims=True))
    r = jnp.concatenate(r_rows, axis=0)
    q = jnp.transpose(qcol[...])[:heads]

    first = me_s == 0
    for k in range(n_head):
        part_copies[2 * k].wait_recv()
    far_pre = bias
    for k in range(n_head):
        far_pre = far_pre + part_far[2 * k]
    far_dt = softplus(far_pre)
    far_cum = exact_mm(-rate * far_dt, summing)
    far_total = far_cum[:, tokens - 1 :]
    from_start = jnp.exp(cum)
    to_end = jnp.exp(total - cum)
    far_scale = jnp.where(first, jnp.exp(far_cum), jnp.exp(far_total - far_cum) * far_dt)
    near_scale = jnp.where(first, to_end * dt, from_start)
    far_wide = widen(far_scale)
    near_wide = widen(near_scale)
    for copy in raw_copies:
        copy.wait_recv()
    state = mm(
        far_bc[...], (far_xg[...].astype(jnp.float32) * far_wide).astype(jnp.bfloat16), TN
    ).astype(jnp.bfloat16)
    carried = mm(bc[me_s], state, NN)
    near = xg[me_s].astype(jnp.float32)
    high, low = two_parts(near * carried)
    w = mm(spread[:heads], high, NT) + mm(spread[:heads], low, NT)

    v = to_end * w
    q = jnp.where(first, q + v, q)
    da = r - dt * q + jnp.where(first, 0.0, from_start * w)
    at_end = jnp.where(first, jnp.sum(dt * v, axis=1, keepdims=True), 0.0)
    lower = (
        lax.broadcasted_iota(jnp.int32, (tokens, tokens), 0)
        >= lax.broadcasted_iota(jnp.int32, (tokens, tokens), 1)
    ).astype(jnp.float32)
    grad_step = q - rate * (exact_mm(da, lower) + at_end)
    my_rows = pl.ds(pl.multiple_of(me_h * heads, heads), heads)
    gp_all[my_rows, :] = (grad_step * jax.nn.sigmoid(preact)).astype(jnp.bfloat16)
    gp_copies = []
    for k in range(1, n_head):
        copy = pltpu.make_async_remote_copy(
            src_ref=gp_all.at[my_rows],
            dst_ref=gp_all.at[my_rows],
            send_sem=g_send.at[k - 1],
            recv_sem=g_recv.at[k - 1],
            device_id=place(me_s, head_at(k), me_d),
            device_id_type=MESH,
        )
        copy.start()
        gp_copies.append(copy)

    dt_wide = widen(dt)
    flag = jnp.where(first, 1.0, 0.0)
    for j in range(heads // 2):
        lanes = slice(j * pair, (j + 1) * pair)
        gy_pair = xg[1, :, lanes]
        inner = jnp.where(left, mm(ke[2 * j], gy_pair, NN), mm(ke[2 * j + 1], gy_pair, NN))
        gx_ref[:, lanes] = (
            inner * dt_wide[:, lanes] + flag * near_wide[:, lanes] * carried[:, lanes]
        ).astype(jnp.bfloat16)
    extra = mm((near * near_wide).astype(jnp.bfloat16), state, NT)
    dk = dkt.astype(jnp.bfloat16)
    gb_ref[...] = (mm(dk, bc[1], NN) + flag * extra).astype(jnp.bfloat16)
    gc_ref[...] = (mm(dk, bc[0], TN) + (1.0 - flag) * extra).astype(jnp.bfloat16)

    for copy in gp_copies:
        copy.wait_recv()
    gw_send[...] = mm(gp_all[...], layer[...], NN).astype(jnp.bfloat16)
    gw_copies = []
    for cut in range(cuts):
        row = me_h * cuts + cut
        to_s, to_d = row // n_dp, lax.rem(row, n_dp)
        for k in range(n_head):
            to = head_at(k)
            at = cut * n_head + k
            block = gw_send.at[
                pl.ds(pl.multiple_of(to * heads, heads), heads),
                cut * rows_out : (cut + 1) * rows_out,
            ]
            copy = pltpu.make_async_remote_copy(
                src_ref=block,
                dst_ref=gw_recv.at[my_row],
                send_sem=d_send.at[at],
                recv_sem=d_recv.at[my_row],
                device_id=place(to_s, to, to_d),
                device_id_type=MESH,
            )
            if k:
                copy.start()
                gw_copies.append((copy, None))
            else:
                away = row != my_row
                pl.when(away)(copy.start)
                gw_copies.append((copy, away))

                @pl.when(jnp.logical_not(away))
                def _():
                    gw_recv[my_row] = block[...]

    gin = jnp.zeros((tokens, feats), jnp.float32)
    for j in range(n_head):
        rows = slice(j * heads, (j + 1) * heads)
        term = mm(gp_all[rows, :], w_all[rows, :], TN)
        gin = gin + term.astype(jnp.bfloat16).astype(jnp.float32)
    gin_ref[...] = gin.astype(jnp.bfloat16)

    def arrived(k):
        spot = lax.rem(my_row + k, share)
        return pltpu.make_async_remote_copy(
            src_ref=gw_recv.at[spot],
            dst_ref=gw_recv.at[spot],
            send_sem=d_send.at[0],
            recv_sem=d_recv.at[spot],
            device_id=place(far_s, me_h, me_d),
            device_id_type=MESH,
        )

    for k in range(1, share):
        arrived(k).wait_recv()
    pl.when(jnp.logical_not(mine))(arrived(0).wait_recv)
    gw = gw_recv[0].astype(jnp.float32)
    for k in range(1, share):
        gw = gw + gw_recv[k].astype(jnp.float32)
    gw_ref[...] = gw

    for copy in w_copies + raw_copies + part_copies + gp_copies:
        copy.wait_send()
    for copy, away in gw_copies:
        if away is None:
            copy.wait_send()
        else:
            pl.when(away)(copy.wait_send)


def fused_body(
    mesh, layer_input, head_input, in_matrix, out_matrix, grad_output, step_weight, step_bias, decay_log
):
    n_seq, n_head, n_dp = (mesh.shape[a] for a in ("seq", "head", "dp"))
    tokens, feats = layer_input.shape[1:]
    width = head_input.shape[2]
    state_size = in_matrix.shape[2]
    heads = step_bias.shape[0]
    rows_out = step_weight.shape[0] // (n_seq * n_dp)
    share = n_seq * n_dp
    b16, f32 = jnp.bfloat16, jnp.float32
    dma = pltpu.SemaphoreType.DMA
    hbm = pl.BlockSpec(memory_space=pl.ANY)
    vmem = pl.BlockSpec(memory_space=pltpu.VMEM)
    gx, gb, gc, gin, gw = pl.pallas_call(
        functools.partial(mixer_kernel, (n_seq, n_head, n_dp, heads, width // heads)),
        out_shape=(
            jax.ShapeDtypeStruct((tokens, width), b16),
            jax.ShapeDtypeStruct((tokens, state_size), b16),
            jax.ShapeDtypeStruct((tokens, state_size), b16),
            jax.ShapeDtypeStruct((tokens, feats), b16),
            jax.ShapeDtypeStruct((heads, rows_out), f32),
        ),
        in_specs=[hbm] * 6 + [vmem] * 2,
        out_specs=[vmem] * 5,
        scratch_shapes=[
            pltpu.VMEM((tokens, feats), b16),
            pltpu.VMEM((2, tokens, width), b16),
            pltpu.VMEM((2, tokens, state_size), b16),
            pltpu.VMEM((tokens, width), b16),
            pltpu.VMEM((tokens, state_size), b16),
            pltpu.VMEM((n_head * heads, feats), b16),
            pltpu.VMEM((n_head * heads, tokens), f32),
            pltpu.VMEM((2 * n_head - 1, heads, tokens), f32),
            pltpu.VMEM((heads, tokens, tokens), f32),
            pltpu.VMEM((heads, tokens, tokens), b16),
            pltpu.VMEM((tokens, tokens), f32),
            pltpu.VMEM((n_head * heads, tokens), b16),
            pltpu.VMEM((n_head * heads, feats), b16),
            pltpu.VMEM((share, heads, rows_out), b16),
            dma((6,)),
            dma((n_head - 1,)),
            dma((n_head - 1,)),
            dma((2,)),
            dma((2,)),
            dma((2 * n_head - 1,)),
            dma((2 * n_head - 1,)),
            dma((n_head - 1,)),
            dma((n_head - 1,)),
            dma((share,)),
            dma((share,)),
        ],
        compiler_params=pltpu.CompilerParams(
            collective_id=0, has_side_effects=True, vmem_limit_bytes=32 * 1024 * 1024
        ),
        name="mixer",
    )(
        layer_input[0], head_input[0], in_matrix[0], out_matrix[0], grad_output[0],
        jnp.transpose(step_weight), step_bias[None], decay_log[None],
    )
    return gx[None], gb[None], gc[None], gin[None], jnp.transpose(gw)


def fits(mesh, args):
    n_seq, n_head, n_dp = (mesh.shape[a] for a in ("seq", "head", "dp"))
    tokens = args[0].shape[1] // n_seq
    return (
        n_seq == 2
        and n_head == G
        and tokens == BLOCK
        and (n_seq * n_dp) % n_head == 0
    )


def solution(mesh):
    in_specs = (
        P("dp", "seq", "head"),
        P("dp", "seq", "head"),
        P("dp", "seq", "head"),
        P("dp", "seq", "head"),
        P("dp", "seq", "head"),
        P(None, "head"),
        P("head"),
        P("head"),
    )
    out_specs = (
        P("dp", "seq", "head"),
        P("dp", "seq", "head"),
        P("dp", "seq", "head"),
        P("dp", "seq", "head"),
        P(("seq", "dp"), "head"),
    )

    def run(*args):
        here = functools.partial(fused_body, mesh) if fits(mesh, args) else body
        return jax.shard_map(
            here, mesh=mesh, in_specs=in_specs, out_specs=out_specs, check_vma=False
        )(*args)

    return run
```

```python
import functools

import jax
import jax.numpy as jnp
from jax import lax
from jax.experimental import pallas as pl
from jax.experimental.pallas import tpu as pltpu
from jax.sharding import PartitionSpec as P

H = 64
P_SIZE = 64
NSTATE = 128
G = 4
BLOCK = 128


PRECISION_LEVEL = lax.Precision.HIGHEST


def prefix(value, axis, join, neutral, backward):
    count = lax.axis_size(axis)
    place = lax.axis_index(axis)
    ahead = count - 1 - place if backward else place
    gathered = jax.tree.map(
        lambda a, kind: lax.all_gather(a.astype(kind), axis), value, (jnp.bfloat16, jnp.bfloat16)
    )
    state = jax.tree.map(lambda a, e: jnp.zeros_like(a) + jnp.asarray(e, a.dtype), value, neutral)

    def one(step, state):
        source = count - 1 - step if backward else step
        return join(
            state,
            jax.tree.map(
                lambda a, own: lax.dynamic_index_in_dim(a, source, 0, False).astype(own.dtype),
                gathered,
                value,
            ),
        )

    return lax.fori_loop(0, ahead, one, state)


def block_step(carry_state, inputs):
    input_block, b_block, c_block, step_block, decay_block = inputs
    cumulated = jnp.cumsum(decay_block, axis=-1)
    block_len = cumulated.shape[-1]
    lower_mask = jnp.arange(block_len)[:, None] >= jnp.arange(block_len)[None, :]
    decay_span = jnp.exp(
        jnp.where(lower_mask, cumulated[..., :, None] - cumulated[..., None, :], -1e30)
    )
    kernel = jnp.einsum("tgn,sgn->gts", c_block, b_block, precision=PRECISION_LEVEL)
    weight_values = kernel[:, None] * decay_span * step_block[..., None, :]
    within_block = jnp.einsum(
        "idwz,zidx->widx", weight_values, input_block, precision=PRECISION_LEVEL
    )
    carried = jnp.einsum("tgn,grnp->tgrp", c_block, carry_state, precision=PRECISION_LEVEL)
    output = within_block + jnp.moveaxis(jnp.exp(cumulated), -1, 0)[..., None] * carried
    totals = cumulated[..., -1]
    inflow = jnp.exp(totals[..., None] - cumulated) * step_block
    fresh_term = jnp.einsum(
        "grs,sgn,sgrp->grnp", inflow, b_block, input_block, precision=PRECISION_LEVEL
    )
    return (jnp.exp(totals)[..., None, None] * carry_state + fresh_term, output)


def segment(x_rows, b_rows, readout_rows, step_sizes, decays, start_state):
    length = x_rows.shape[0]
    blocks = length // BLOCK

    def split_rows(values):
        return values.reshape((blocks, BLOCK) + values.shape[1:])

    def split_last(values):
        return jnp.moveaxis(values.reshape(values.shape[:-1] + (blocks, BLOCK)), -2, 0)

    final_state, outputs = lax.scan(
        block_step,
        start_state,
        (
            split_rows(x_rows),
            split_rows(b_rows),
            split_rows(readout_rows),
            split_last(step_sizes),
            split_last(decays),
        ),
    )
    return (outputs.reshape(x_rows.shape), final_state)


def join_pairs(earlier, later):
    return (earlier[0] + later[0], jnp.exp(later[0])[..., None, None] * earlier[1] + later[1])


def body(
    layer_input, head_input, in_matrix, out_matrix, grad_output, step_weight, step_bias, decay_log
):
    tokens = head_input.shape[1]
    group_count = in_matrix.shape[2] // NSTATE
    ratio = H // G
    heads_here = group_count * ratio
    whole_input = lax.all_gather(layer_input, "head", axis=2, tiled=True)[0]
    preact = jnp.dot(whole_input, step_weight, preferred_element_type=jnp.float32) + step_bias
    step_sizes = jnp.transpose(jax.nn.softplus(preact)).reshape(group_count, ratio, tokens)
    rates = jnp.exp(decay_log).reshape(group_count, ratio)
    decays = -rates[..., None] * step_sizes
    x_rows = head_input[0].astype(jnp.float32).reshape(tokens, group_count, ratio, P_SIZE)
    b_rows = in_matrix[0].astype(jnp.float32).reshape(tokens, group_count, NSTATE)
    readout_rows = out_matrix[0].astype(jnp.float32).reshape(tokens, group_count, NSTATE)
    output_gradient = grad_output[0].astype(jnp.float32).reshape(tokens, group_count, ratio, P_SIZE)
    running_state = jnp.cumsum(decays, axis=-1)
    totals = running_state[..., -1]
    local_state = jnp.einsum(
        "grs,sgn,sgrp->grnp",
        jnp.exp(totals[..., None] - running_state) * step_sizes,
        b_rows,
        x_rows,
        precision=PRECISION_LEVEL,
    )
    local_grad = jnp.einsum(
        "vad,dvm,dvah->vamh",
        jnp.exp(running_state),
        readout_rows,
        output_gradient,
        precision=PRECISION_LEVEL,
    )
    neutral = (jnp.zeros_like(totals), jnp.zeros_like(local_state))
    incoming = prefix((totals, local_state), "seq", join_pairs, neutral, False)[1]
    outgoing = prefix((totals, local_grad), "seq", join_pairs, neutral, True)[1]

    def local_map(x_arg, b_arg, c_arg, step_arg):
        return segment(x_arg, b_arg, c_arg, step_arg, -rates[..., None] * step_arg, incoming)

    forward_out, pullback = jax.vjp(local_map, x_rows, b_rows, readout_rows, step_sizes)
    grad_x, grad_b, grad_c, grad_step = pullback((output_gradient, outgoing))
    grad_pre = (
        jnp.transpose(grad_step.reshape(heads_here, tokens)) * jax.nn.sigmoid(preact)
    ).astype(jnp.bfloat16)
    partial_terms = lax.dot_general(
        grad_pre, step_weight, (((1,), (1,)), ((), ())), preferred_element_type=jnp.float32
    )
    grad_input = lax.psum_scatter(
        partial_terms.astype(jnp.bfloat16), "head", scatter_dimension=1, tiled=True
    )
    seq_part = lax.psum_scatter(
        lax.dot_general(
            whole_input, grad_pre, (((0,), (0,)), ((), ())), preferred_element_type=jnp.float32
        ).astype(jnp.bfloat16),
        "seq",
        scatter_dimension=0,
        tiled=True,
    ).astype(jnp.float32)
    grad_weight = lax.psum_scatter(seq_part, "dp", scatter_dimension=0, tiled=True)
    return (
        grad_x.reshape(tokens, heads_here * P_SIZE).astype(jnp.bfloat16)[None],
        grad_b.reshape(tokens, group_count * NSTATE).astype(jnp.bfloat16)[None],
        grad_c.reshape(tokens, group_count * NSTATE).astype(jnp.bfloat16)[None],
        grad_input[None],
        grad_weight,
    )


MESH = pl.DeviceIdType.MESH
CHUNKS = 4
NT = (((1,), (1,)), ((), ()))
NN = (((1,), (0,)), ((), ()))
TN = (((0,), (0,)), ((), ()))


def mm(a, b, dims):
    return lax.dot_general(a, b, dims, preferred_element_type=jnp.float32)


def exact_mm(a, b):
    return lax.dot_general(
        a, b, NN, precision=lax.Precision.HIGHEST, preferred_element_type=jnp.float32
    )


def two_parts(v):
    high = v.astype(jnp.bfloat16)
    low = (v - high.astype(jnp.float32)).astype(jnp.bfloat16)
    return high, low


def softplus(v):
    return jnp.maximum(v, 0.0) + jnp.log1p(jnp.exp(-jnp.abs(v)))


def mixer_kernel(
    sizes,
    layer_hbm, x_hbm, b_hbm, c_hbm, gy_hbm, w_hbm, bias_hbm, rate_hbm,
    gx_hbm, gb_hbm, gc_hbm, gin_hbm, gw_hbm,
    gx_ref, gb_ref, gc_ref, gin_ref, gw_ref, out_sem,
    bias_ref, rate_ref, layer, xg, bc, far_xg, far_bc, w_all, part, part_far, mt, ke, qcol, gp_all, gw_send, gw_recv,
    load_sem, w_send, w_recv, raw_send, raw_recv, p_send, p_recv, g_send, g_recv, d_send, d_recv,
):
    n_seq, n_head, n_dp, heads, p_size = sizes
    tokens, feats = layer.shape
    me_s, me_h, me_d = lax.axis_index("seq"), lax.axis_index("head"), lax.axis_index("dp")
    far_s = 1 - me_s
    rows_out = gw_ref.shape[1]
    cuts = feats // rows_out
    share = n_seq * n_dp

    def head_at(k):
        return lax.rem(me_h + k, n_head)

    def place(s, h, d):
        return {"seq": s, "head": h, "dp": d}

    stores = [
        pltpu.make_async_copy(src, dst, out_sem.at[at])
        for at, (src, dst) in enumerate(
            (
                (gx_ref, gx_hbm),
                (gb_ref, gb_hbm),
                (gc_ref, gc_hbm),
                (gin_ref, gin_hbm),
                (gw_ref, gw_hbm),
            )
        )
    ]

    loads = [
        pltpu.make_async_copy(x_hbm, xg.at[0], load_sem.at[0]),
        pltpu.make_async_copy(gy_hbm, xg.at[1], load_sem.at[1]),
        pltpu.make_async_copy(b_hbm, bc.at[0], load_sem.at[2]),
        pltpu.make_async_copy(c_hbm, bc.at[1], load_sem.at[3]),
        pltpu.make_async_copy(layer_hbm, layer, load_sem.at[4]),
        pltpu.make_async_copy(
            w_hbm.at[:, pl.ds(pl.multiple_of(me_h * feats, feats), feats)],
            w_all.at[pl.ds(pl.multiple_of(me_h * heads, heads), heads)],
            load_sem.at[5],
        ),
        pltpu.make_async_copy(bias_hbm, bias_ref, load_sem.at[6]),
        pltpu.make_async_copy(rate_hbm, rate_ref, load_sem.at[7]),
    ]
    for load in loads:
        load.start()

    barrier = pltpu.get_barrier_semaphore()
    my_row = me_s * n_dp + me_d
    source_h = my_row // cuts
    for k in range(n_head):
        if k:
            pl.semaphore_signal(
                barrier, inc=1, device_id=place(me_s, head_at(k), me_d), device_id_type=MESH
            )
        pl.semaphore_signal(
            barrier, inc=1, device_id=place(far_s, head_at(k), me_d), device_id_type=MESH
        )
    mine = source_h == me_h
    for k in range(share):
        spot = lax.rem(my_row + k, share)

        def greet():
            pl.semaphore_signal(
                barrier,
                inc=1,
                device_id=place(spot // n_dp, source_h, lax.rem(spot, n_dp)),
                device_id_type=MESH,
            )

        if k:
            greet()
        else:
            pl.when(jnp.logical_not(mine))(greet)
    pl.semaphore_wait(barrier, 2 * n_head - 1 + share - jnp.where(mine, 1, 0))

    w_copies = []
    for k in range(1, n_head):
        to = head_at(k)
        copy = pltpu.make_async_remote_copy(
            src_ref=w_hbm.at[:, pl.ds(pl.multiple_of(to * feats, feats), feats)],
            dst_ref=w_all.at[pl.ds(pl.multiple_of(me_h * heads, heads), heads)],
            send_sem=w_send.at[k - 1],
            recv_sem=w_recv.at[k - 1],
            device_id=place(me_s, to, me_d),
            device_id_type=MESH,
        )
        copy.start()
        w_copies.append(copy)

    for load in loads[:4]:
        load.wait()
    raw_copies = []
    width = far_xg.shape[1] // CHUNKS
    chunks = [slice(c * width, (c + 1) * width) for c in range(CHUNKS)]
    near_refs = [bc.at[me_s]] + [xg.at[me_s, :, lanes] for lanes in chunks]
    far_refs = [far_bc] + [far_xg.at[:, lanes] for lanes in chunks]
    for at in range(CHUNKS + 1):
        copy = pltpu.make_async_remote_copy(
            src_ref=near_refs[at],
            dst_ref=far_refs[at],
            send_sem=raw_send.at[at],
            recv_sem=raw_recv.at[at],
            device_id=place(far_s, me_h, me_d),
            device_id_type=MESH,
        )
        copy.start()
        raw_copies.append(copy)

    pair = 2 * p_size
    left = lax.broadcasted_iota(jnp.int32, (tokens, pair), 1) < p_size
    kt = mm(bc[0], bc[1], NT)
    zero_pair = jnp.zeros((tokens, pair), jnp.bfloat16)
    for j in range(heads // 2):
        lanes = slice(j * pair, (j + 1) * pair)
        x_pair, gy_pair = xg[0, :, lanes], xg[1, :, lanes]
        mt[2 * j] = mm(jnp.where(left, x_pair, zero_pair), gy_pair, NT)
        mt[2 * j + 1] = mm(jnp.where(left, zero_pair, x_pair), gy_pair, NT)

    for load in loads[4:]:
        load.wait()
    for copy in w_copies:
        copy.wait_recv()
    part[...] = mm(w_all[...], layer[...], NT)
    part_copies = []
    for k in range(n_head):
        to = head_at(k)
        for hop in range(2):
            if k == 0 and hop == 0:
                continue
            at = 2 * k + hop - 1
            copy = pltpu.make_async_remote_copy(
                src_ref=part.at[pl.ds(pl.multiple_of(to * heads, heads), heads)],
                dst_ref=part_far.at[at],
                send_sem=p_send.at[at],
                recv_sem=p_recv.at[at],
                device_id=place(far_s if hop else me_s, to, me_d),
                device_id_type=MESH,
            )
            copy.start()
            part_copies.append(copy)

    upper = (
        lax.broadcasted_iota(jnp.int32, (tokens, tokens), 0)
        <= lax.broadcasted_iota(jnp.int32, (tokens, tokens), 1)
    )
    summing = upper.astype(jnp.float32)
    square = lax.broadcasted_iota(jnp.int32, (heads, heads), 0) == lax.broadcasted_iota(
        jnp.int32, (heads, heads), 1
    )

    def column(row):
        return jnp.sum(jnp.where(square, row, 0.0), axis=1, keepdims=True)

    bias = column(bias_ref[...])
    rate = jnp.exp(column(rate_ref[...]))
    spread_rows = lax.rem(lax.broadcasted_iota(jnp.int32, (2 * heads, heads * p_size), 0), heads)
    spread_at = lax.broadcasted_iota(jnp.int32, (2 * heads, heads * p_size), 1) // p_size
    spread = jnp.where(spread_rows == spread_at, 1.0, 0.0).astype(jnp.bfloat16)

    def widen(v):
        high, low = two_parts(v)
        return mm(jnp.concatenate([high, low], axis=0), spread, TN)

    for k in range(1, n_head):
        part_copies[2 * k - 1].wait_recv()
    preact = part[pl.ds(pl.multiple_of(me_h * heads, heads), heads), :] + bias
    for k in range(1, n_head):
        preact = preact + part_far[2 * k - 1]
    dt = softplus(preact)
    cum = exact_mm(-rate * dt, summing)
    total = cum[:, tokens - 1 :]
    cum_col = jnp.transpose(cum)
    dt_col = jnp.transpose(dt)
    dkt = jnp.zeros((tokens, tokens), jnp.float32)
    r_rows = []
    for h in range(heads):
        gap = cum[h : h + 1, :] - cum_col[:, h : h + 1]
        span = jnp.exp(jnp.where(upper, gap, -1e30))
        ke[h] = (kt * span).astype(jnp.bfloat16)
        step_here = dt_col[:, h : h + 1]
        f = mt[h] * span
        dkt = dkt + f * step_here
        prod = f * kt
        qcol[:, h : h + 1] = jnp.sum(prod, axis=1, keepdims=True)
        r_rows.append(jnp.sum(prod * step_here, axis=0, keepdims=True))
    r = jnp.concatenate(r_rows, axis=0)
    q = jnp.transpose(qcol[...])[:heads]

    first = me_s == 0
    for k in range(n_head):
        part_copies[2 * k].wait_recv()
    far_pre = bias
    for k in range(n_head):
        far_pre = far_pre + part_far[2 * k]
    far_dt = softplus(far_pre)
    far_cum = exact_mm(-rate * far_dt, summing)
    far_total = far_cum[:, tokens - 1 :]
    from_start = jnp.exp(cum)
    to_end = jnp.exp(total - cum)
    far_scale = jnp.where(first, jnp.exp(far_cum), jnp.exp(far_total - far_cum) * far_dt)
    near_scale = jnp.where(first, to_end * dt, from_start)
    far_wide = widen(far_scale)
    near_wide = widen(near_scale)
    raw_copies[0].wait_recv()
    far_rows = far_bc[...]
    near_rows = bc[me_s]
    states, carried, inputs = [], [], []
    w = jnp.zeros((heads, tokens), jnp.float32)
    for c, lanes in enumerate(chunks):
        raw_copies[c + 1].wait_recv()
        scaled = far_xg[:, lanes].astype(jnp.float32) * far_wide[:, lanes]
        states.append(mm(far_rows, scaled.astype(jnp.bfloat16), TN).astype(jnp.bfloat16))
        carried.append(mm(near_rows, states[c], NN))
        inputs.append(xg[me_s, :, lanes].astype(jnp.float32))
        high, low = two_parts(inputs[c] * carried[c])
        w = w + mm(spread[:heads, lanes], high, NT) + mm(spread[:heads, lanes], low, NT)

    v = to_end * w
    q = jnp.where(first, q + v, q)
    da = r - dt * q + jnp.where(first, 0.0, from_start * w)
    at_end = jnp.where(first, jnp.sum(dt * v, axis=1, keepdims=True), 0.0)
    lower = (
        lax.broadcasted_iota(jnp.int32, (tokens, tokens), 0)
        >= lax.broadcasted_iota(jnp.int32, (tokens, tokens), 1)
    ).astype(jnp.float32)
    grad_step = q - rate * (exact_mm(da, lower) + at_end)
    my_rows = pl.ds(pl.multiple_of(me_h * heads, heads), heads)
    gp_all[my_rows, :] = (grad_step * jax.nn.sigmoid(preact)).astype(jnp.bfloat16)
    gp_copies = []
    for k in range(1, n_head):
        copy = pltpu.make_async_remote_copy(
            src_ref=gp_all.at[my_rows],
            dst_ref=gp_all.at[my_rows],
            send_sem=g_send.at[k - 1],
            recv_sem=g_recv.at[k - 1],
            device_id=place(me_s, head_at(k), me_d),
            device_id_type=MESH,
        )
        copy.start()
        gp_copies.append(copy)

    dt_wide = widen(dt)
    flag = jnp.where(first, 1.0, 0.0)
    brought = jnp.concatenate(carried, axis=1)
    for j in range(heads // 2):
        lanes = slice(j * pair, (j + 1) * pair)
        gy_pair = xg[1, :, lanes]
        inner = jnp.where(left, mm(ke[2 * j], gy_pair, NN), mm(ke[2 * j + 1], gy_pair, NN))
        gx_ref[:, lanes] = (
            inner * dt_wide[:, lanes] + flag * near_wide[:, lanes] * brought[:, lanes]
        ).astype(jnp.bfloat16)
    extra = jnp.zeros_like(dkt)
    for c, lanes in enumerate(chunks):
        extra = extra + mm((inputs[c] * near_wide[:, lanes]).astype(jnp.bfloat16), states[c], NT)
    dk = dkt.astype(jnp.bfloat16)
    gb_ref[...] = (mm(dk, bc[1], NN) + flag * extra).astype(jnp.bfloat16)
    gc_ref[...] = (mm(dk, bc[0], TN) + (1.0 - flag) * extra).astype(jnp.bfloat16)

    for store in stores[:3]:
        store.start()

    for copy in gp_copies:
        copy.wait_recv()
    gw_send[...] = mm(gp_all[...], layer[...], NN).astype(jnp.bfloat16)
    gw_copies = []
    for cut in range(cuts):
        row = me_h * cuts + cut
        to_s, to_d = row // n_dp, lax.rem(row, n_dp)
        for k in range(n_head):
            to = head_at(k)
            at = cut * n_head + k
            block = gw_send.at[
                pl.ds(pl.multiple_of(to * heads, heads), heads),
                cut * rows_out : (cut + 1) * rows_out,
            ]
            copy = pltpu.make_async_remote_copy(
                src_ref=block,
                dst_ref=gw_recv.at[my_row],
                send_sem=d_send.at[at],
                recv_sem=d_recv.at[my_row],
                device_id=place(to_s, to, to_d),
                device_id_type=MESH,
            )
            if k:
                copy.start()
                gw_copies.append((copy, None))
            else:
                away = row != my_row
                pl.when(away)(copy.start)
                gw_copies.append((copy, away))

                @pl.when(jnp.logical_not(away))
                def _():
                    gw_recv[my_row] = block[...]

    gin = jnp.zeros((tokens, feats), jnp.float32)
    for j in range(n_head):
        rows = slice(j * heads, (j + 1) * heads)
        term = mm(gp_all[rows, :], w_all[rows, :], TN)
        gin = gin + term.astype(jnp.bfloat16).astype(jnp.float32)
    gin_ref[...] = gin.astype(jnp.bfloat16)
    stores[3].start()

    def arrived(k):
        spot = lax.rem(my_row + k, share)
        return pltpu.make_async_remote_copy(
            src_ref=gw_recv.at[spot],
            dst_ref=gw_recv.at[spot],
            send_sem=d_send.at[0],
            recv_sem=d_recv.at[spot],
            device_id=place(far_s, me_h, me_d),
            device_id_type=MESH,
        )

    for k in range(1, share):
        arrived(k).wait_recv()
    pl.when(jnp.logical_not(mine))(arrived(0).wait_recv)
    gw = gw_recv[0].astype(jnp.float32)
    for k in range(1, share):
        gw = gw + gw_recv[k].astype(jnp.float32)
    gw_ref[...] = gw
    stores[4].start()

    for copy in w_copies + raw_copies + part_copies + gp_copies:
        copy.wait_send()
    for copy, away in gw_copies:
        if away is None:
            copy.wait_send()
        else:
            pl.when(away)(copy.wait_send)
    for store in stores:
        store.wait()


def write_out(*refs):
    sems = refs[-1]
    count = len(refs) // 2
    copies = [
        pltpu.make_async_copy(refs[i], refs[count + i], sems.at[i]) for i in range(count)
    ]
    for copy in copies:
        copy.start()
    for copy in copies:
        copy.wait()


def fused_body(
    mesh, layer_input, head_input, in_matrix, out_matrix, grad_output, step_weight, step_bias, decay_log
):
    n_seq, n_head, n_dp = (mesh.shape[a] for a in ("seq", "head", "dp"))
    tokens, feats = layer_input.shape[1:]
    width = head_input.shape[2]
    state_size = in_matrix.shape[2]
    heads = step_bias.shape[0]
    rows_out = step_weight.shape[0] // (n_seq * n_dp)
    share = n_seq * n_dp
    b16, f32 = jnp.bfloat16, jnp.float32
    dma = pltpu.SemaphoreType.DMA
    hbm = pl.BlockSpec(memory_space=pltpu.HBM)
    results = pl.pallas_call(
        functools.partial(mixer_kernel, (n_seq, n_head, n_dp, heads, width // heads)),
        out_shape=(
            jax.ShapeDtypeStruct((tokens, width), b16),
            jax.ShapeDtypeStruct((tokens, state_size), b16),
            jax.ShapeDtypeStruct((tokens, state_size), b16),
            jax.ShapeDtypeStruct((tokens, feats), b16),
            jax.ShapeDtypeStruct((heads, rows_out), f32),
        ),
        in_specs=[hbm] * 8,
        out_specs=[hbm] * 5,
        scratch_shapes=[
            pltpu.VMEM((tokens, width), b16),
            pltpu.VMEM((tokens, state_size), b16),
            pltpu.VMEM((tokens, state_size), b16),
            pltpu.VMEM((tokens, feats), b16),
            pltpu.VMEM((heads, rows_out), f32),
            dma((5,)),
            pltpu.VMEM((1, heads), f32),
            pltpu.VMEM((1, heads), f32),
            pltpu.VMEM((tokens, feats), b16),
            pltpu.VMEM((2, tokens, width), b16),
            pltpu.VMEM((2, tokens, state_size), b16),
            pltpu.VMEM((tokens, width), b16),
            pltpu.VMEM((tokens, state_size), b16),
            pltpu.VMEM((n_head * heads, feats), b16),
            pltpu.VMEM((n_head * heads, tokens), f32),
            pltpu.VMEM((2 * n_head - 1, heads, tokens), f32),
            pltpu.VMEM((heads, tokens, tokens), f32),
            pltpu.VMEM((heads, tokens, tokens), b16),
            pltpu.VMEM((tokens, tokens), f32),
            pltpu.VMEM((n_head * heads, tokens), b16),
            pltpu.VMEM((n_head * heads, feats), b16),
            pltpu.VMEM((share, heads, rows_out), b16),
            dma((8,)),
            dma((n_head - 1,)),
            dma((n_head - 1,)),
            dma((CHUNKS + 1,)),
            dma((CHUNKS + 1,)),
            dma((2 * n_head - 1,)),
            dma((2 * n_head - 1,)),
            dma((n_head - 1,)),
            dma((n_head - 1,)),
            dma((share,)),
            dma((share,)),
        ],
        compiler_params=pltpu.CompilerParams(
            collective_id=0, has_side_effects=True, vmem_limit_bytes=60 * 1024 * 1024
        ),
        name="mixer",
    )(
        layer_input[0], head_input[0], in_matrix[0], out_matrix[0], grad_output[0],
        jnp.transpose(step_weight), step_bias[None], decay_log[None],
    )
    count = len(results)
    gx, gb, gc, gin, gw = pl.pallas_call(
        write_out,
        out_shape=tuple(jax.ShapeDtypeStruct(a.shape, a.dtype) for a in results),
        in_specs=[pl.BlockSpec(memory_space=pl.ANY)] * count,
        out_specs=[hbm] * count,
        scratch_shapes=[dma((count,))],
        compiler_params=pltpu.CompilerParams(vmem_limit_bytes=60 * 1024 * 1024),
        name="write_out",
    )(*results)
    return gx[None], gb[None], gc[None], gin[None], jnp.transpose(gw)


def fits(mesh, args):
    n_seq, n_head, n_dp = (mesh.shape[a] for a in ("seq", "head", "dp"))
    tokens = args[0].shape[1] // n_seq
    return (
        n_seq == 2
        and n_head == G
        and tokens == BLOCK
        and (n_seq * n_dp) % n_head == 0
    )


def solution(mesh):
    in_specs = (
        P("dp", "seq", "head"),
        P("dp", "seq", "head"),
        P("dp", "seq", "head"),
        P("dp", "seq", "head"),
        P("dp", "seq", "head"),
        P(None, "head"),
        P("head"),
        P("head"),
    )
    out_specs = (
        P("dp", "seq", "head"),
        P("dp", "seq", "head"),
        P("dp", "seq", "head"),
        P("dp", "seq", "head"),
        P(("seq", "dp"), "head"),
    )

    def run(*args):
        here = functools.partial(fused_body, mesh) if fits(mesh, args) else body
        return jax.shard_map(
            here, mesh=mesh, in_specs=in_specs, out_specs=out_specs, check_vma=False
        )(*args)

    return run
```

```python
import functools

import jax
import jax.numpy as jnp
from jax import lax
from jax.experimental import pallas as pl
from jax.experimental.pallas import tpu as pltpu
from jax.sharding import PartitionSpec as P

H = 64
P_SIZE = 64
NSTATE = 128
G = 4
BLOCK = 128


PRECISION_LEVEL = lax.Precision.HIGHEST


def prefix(value, axis, join, neutral, backward):
    count = lax.axis_size(axis)
    place = lax.axis_index(axis)
    ahead = count - 1 - place if backward else place
    gathered = jax.tree.map(
        lambda a, kind: lax.all_gather(a.astype(kind), axis), value, (jnp.bfloat16, jnp.bfloat16)
    )
    state = jax.tree.map(lambda a, e: jnp.zeros_like(a) + jnp.asarray(e, a.dtype), value, neutral)

    def one(step, state):
        source = count - 1 - step if backward else step
        return join(
            state,
            jax.tree.map(
                lambda a, own: lax.dynamic_index_in_dim(a, source, 0, False).astype(own.dtype),
                gathered,
                value,
            ),
        )

    return lax.fori_loop(0, ahead, one, state)


def block_step(carry_state, inputs):
    input_block, b_block, c_block, step_block, decay_block = inputs
    cumulated = jnp.cumsum(decay_block, axis=-1)
    block_len = cumulated.shape[-1]
    lower_mask = jnp.arange(block_len)[:, None] >= jnp.arange(block_len)[None, :]
    decay_span = jnp.exp(
        jnp.where(lower_mask, cumulated[..., :, None] - cumulated[..., None, :], -1e30)
    )
    kernel = jnp.einsum("tgn,sgn->gts", c_block, b_block, precision=PRECISION_LEVEL)
    weight_values = kernel[:, None] * decay_span * step_block[..., None, :]
    within_block = jnp.einsum(
        "idwz,zidx->widx", weight_values, input_block, precision=PRECISION_LEVEL
    )
    carried = jnp.einsum("tgn,grnp->tgrp", c_block, carry_state, precision=PRECISION_LEVEL)
    output = within_block + jnp.moveaxis(jnp.exp(cumulated), -1, 0)[..., None] * carried
    totals = cumulated[..., -1]
    inflow = jnp.exp(totals[..., None] - cumulated) * step_block
    fresh_term = jnp.einsum(
        "grs,sgn,sgrp->grnp", inflow, b_block, input_block, precision=PRECISION_LEVEL
    )
    return (jnp.exp(totals)[..., None, None] * carry_state + fresh_term, output)


def segment(x_rows, b_rows, readout_rows, step_sizes, decays, start_state):
    length = x_rows.shape[0]
    blocks = length // BLOCK

    def split_rows(values):
        return values.reshape((blocks, BLOCK) + values.shape[1:])

    def split_last(values):
        return jnp.moveaxis(values.reshape(values.shape[:-1] + (blocks, BLOCK)), -2, 0)

    final_state, outputs = lax.scan(
        block_step,
        start_state,
        (
            split_rows(x_rows),
            split_rows(b_rows),
            split_rows(readout_rows),
            split_last(step_sizes),
            split_last(decays),
        ),
    )
    return (outputs.reshape(x_rows.shape), final_state)


def join_pairs(earlier, later):
    return (earlier[0] + later[0], jnp.exp(later[0])[..., None, None] * earlier[1] + later[1])


def body(
    layer_input, head_input, in_matrix, out_matrix, grad_output, step_weight, step_bias, decay_log
):
    tokens = head_input.shape[1]
    group_count = in_matrix.shape[2] // NSTATE
    ratio = H // G
    heads_here = group_count * ratio
    whole_input = lax.all_gather(layer_input, "head", axis=2, tiled=True)[0]
    preact = jnp.dot(whole_input, step_weight, preferred_element_type=jnp.float32) + step_bias
    step_sizes = jnp.transpose(jax.nn.softplus(preact)).reshape(group_count, ratio, tokens)
    rates = jnp.exp(decay_log).reshape(group_count, ratio)
    decays = -rates[..., None] * step_sizes
    x_rows = head_input[0].astype(jnp.float32).reshape(tokens, group_count, ratio, P_SIZE)
    b_rows = in_matrix[0].astype(jnp.float32).reshape(tokens, group_count, NSTATE)
    readout_rows = out_matrix[0].astype(jnp.float32).reshape(tokens, group_count, NSTATE)
    output_gradient = grad_output[0].astype(jnp.float32).reshape(tokens, group_count, ratio, P_SIZE)
    running_state = jnp.cumsum(decays, axis=-1)
    totals = running_state[..., -1]
    local_state = jnp.einsum(
        "grs,sgn,sgrp->grnp",
        jnp.exp(totals[..., None] - running_state) * step_sizes,
        b_rows,
        x_rows,
        precision=PRECISION_LEVEL,
    )
    local_grad = jnp.einsum(
        "vad,dvm,dvah->vamh",
        jnp.exp(running_state),
        readout_rows,
        output_gradient,
        precision=PRECISION_LEVEL,
    )
    neutral = (jnp.zeros_like(totals), jnp.zeros_like(local_state))
    incoming = prefix((totals, local_state), "seq", join_pairs, neutral, False)[1]
    outgoing = prefix((totals, local_grad), "seq", join_pairs, neutral, True)[1]

    def local_map(x_arg, b_arg, c_arg, step_arg):
        return segment(x_arg, b_arg, c_arg, step_arg, -rates[..., None] * step_arg, incoming)

    forward_out, pullback = jax.vjp(local_map, x_rows, b_rows, readout_rows, step_sizes)
    grad_x, grad_b, grad_c, grad_step = pullback((output_gradient, outgoing))
    grad_pre = (
        jnp.transpose(grad_step.reshape(heads_here, tokens)) * jax.nn.sigmoid(preact)
    ).astype(jnp.bfloat16)
    partial_terms = lax.dot_general(
        grad_pre, step_weight, (((1,), (1,)), ((), ())), preferred_element_type=jnp.float32
    )
    grad_input = lax.psum_scatter(
        partial_terms.astype(jnp.bfloat16), "head", scatter_dimension=1, tiled=True
    )
    seq_part = lax.psum_scatter(
        lax.dot_general(
            whole_input, grad_pre, (((0,), (0,)), ((), ())), preferred_element_type=jnp.float32
        ).astype(jnp.bfloat16),
        "seq",
        scatter_dimension=0,
        tiled=True,
    ).astype(jnp.float32)
    grad_weight = lax.psum_scatter(seq_part, "dp", scatter_dimension=0, tiled=True)
    return (
        grad_x.reshape(tokens, heads_here * P_SIZE).astype(jnp.bfloat16)[None],
        grad_b.reshape(tokens, group_count * NSTATE).astype(jnp.bfloat16)[None],
        grad_c.reshape(tokens, group_count * NSTATE).astype(jnp.bfloat16)[None],
        grad_input[None],
        grad_weight,
    )


MESH = pl.DeviceIdType.MESH
CHUNKS = 4
NT = (((1,), (1,)), ((), ()))
NN = (((1,), (0,)), ((), ()))
TN = (((0,), (0,)), ((), ()))


def mm(a, b, dims):
    return lax.dot_general(a, b, dims, preferred_element_type=jnp.float32)


def exact_mm(a, b):
    return lax.dot_general(
        a, b, NN, precision=lax.Precision.HIGHEST, preferred_element_type=jnp.float32
    )


def two_parts(v):
    high = v.astype(jnp.bfloat16)
    low = (v - high.astype(jnp.float32)).astype(jnp.bfloat16)
    return high, low


def softplus(v):
    return jnp.maximum(v, 0.0) + jnp.log1p(jnp.exp(-jnp.abs(v)))


def mixer_kernel(
    sizes,
    layer_hbm, x_hbm, b_hbm, c_hbm, gy_hbm, w_hbm, bias_hbm, rate_hbm,
    gx_ref, gb_ref, gc_ref, gin_ref, gw_ref,
    bias_ref, rate_ref, layer, xg, bc, far_xg, far_bc, w_all, part, part_far, mt, ke, qcol, gp_all, gw_send, gw_recv,
    load_sem, w_send, w_recv, raw_send, raw_recv, p_send, p_recv, g_send, g_recv, d_send, d_recv,
):
    n_seq, n_head, n_dp, heads, p_size = sizes
    tokens, feats = layer.shape
    me_s, me_h, me_d = lax.axis_index("seq"), lax.axis_index("head"), lax.axis_index("dp")
    far_s = 1 - me_s
    rows_out = gw_ref.shape[1]
    cuts = feats // rows_out
    share = n_seq * n_dp

    def head_at(k):
        return lax.rem(me_h + k, n_head)

    def place(s, h, d):
        return {"seq": s, "head": h, "dp": d}

    loads = [
        pltpu.make_async_copy(x_hbm, xg.at[0], load_sem.at[0]),
        pltpu.make_async_copy(gy_hbm, xg.at[1], load_sem.at[1]),
        pltpu.make_async_copy(b_hbm, bc.at[0], load_sem.at[2]),
        pltpu.make_async_copy(c_hbm, bc.at[1], load_sem.at[3]),
        pltpu.make_async_copy(layer_hbm, layer, load_sem.at[4]),
        pltpu.make_async_copy(
            w_hbm.at[:, pl.ds(pl.multiple_of(me_h * feats, feats), feats)],
            w_all.at[pl.ds(pl.multiple_of(me_h * heads, heads), heads)],
            load_sem.at[5],
        ),
        pltpu.make_async_copy(bias_hbm, bias_ref, load_sem.at[6]),
        pltpu.make_async_copy(rate_hbm, rate_ref, load_sem.at[7]),
    ]
    for load in loads:
        load.start()

    barrier = pltpu.get_barrier_semaphore()
    my_row = me_s * n_dp + me_d
    source_h = my_row // cuts
    for k in range(n_head):
        if k:
            pl.semaphore_signal(
                barrier, inc=1, device_id=place(me_s, head_at(k), me_d), device_id_type=MESH
            )
        pl.semaphore_signal(
            barrier, inc=1, device_id=place(far_s, head_at(k), me_d), device_id_type=MESH
        )
    mine = source_h == me_h
    for k in range(share):
        spot = lax.rem(my_row + k, share)

        def greet():
            pl.semaphore_signal(
                barrier,
                inc=1,
                device_id=place(spot // n_dp, source_h, lax.rem(spot, n_dp)),
                device_id_type=MESH,
            )

        if k:
            greet()
        else:
            pl.when(jnp.logical_not(mine))(greet)
    pl.semaphore_wait(barrier, 2 * n_head - 1 + share - jnp.where(mine, 1, 0))

    w_copies = []
    for k in range(1, n_head):
        to = head_at(k)
        copy = pltpu.make_async_remote_copy(
            src_ref=w_hbm.at[:, pl.ds(pl.multiple_of(to * feats, feats), feats)],
            dst_ref=w_all.at[pl.ds(pl.multiple_of(me_h * heads, heads), heads)],
            send_sem=w_send.at[k - 1],
            recv_sem=w_recv.at[k - 1],
            device_id=place(me_s, to, me_d),
            device_id_type=MESH,
        )
        copy.start()
        w_copies.append(copy)

    for load in loads[:4]:
        load.wait()
    raw_copies = []
    width = far_xg.shape[1] // CHUNKS
    chunks = [slice(c * width, (c + 1) * width) for c in range(CHUNKS)]
    near_refs = [bc.at[me_s]] + [xg.at[me_s, :, lanes] for lanes in chunks]
    far_refs = [far_bc] + [far_xg.at[:, lanes] for lanes in chunks]
    for at in range(CHUNKS + 1):
        copy = pltpu.make_async_remote_copy(
            src_ref=near_refs[at],
            dst_ref=far_refs[at],
            send_sem=raw_send.at[at],
            recv_sem=raw_recv.at[at],
            device_id=place(far_s, me_h, me_d),
            device_id_type=MESH,
        )
        copy.start()
        raw_copies.append(copy)

    pair = 2 * p_size
    left = lax.broadcasted_iota(jnp.int32, (tokens, pair), 1) < p_size
    kt = mm(bc[0], bc[1], NT)
    zero_pair = jnp.zeros((tokens, pair), jnp.bfloat16)
    for j in range(heads // 2):
        lanes = slice(j * pair, (j + 1) * pair)
        x_pair, gy_pair = xg[0, :, lanes], xg[1, :, lanes]
        mt[2 * j] = mm(jnp.where(left, x_pair, zero_pair), gy_pair, NT)
        mt[2 * j + 1] = mm(jnp.where(left, zero_pair, x_pair), gy_pair, NT)

    for load in loads[4:]:
        load.wait()
    for copy in w_copies:
        copy.wait_recv()
    part[...] = mm(w_all[...], layer[...], NT)
    part_copies = []
    for k in range(n_head):
        to = head_at(k)
        for hop in range(2):
            if k == 0 and hop == 0:
                continue
            at = 2 * k + hop - 1
            copy = pltpu.make_async_remote_copy(
                src_ref=part.at[pl.ds(pl.multiple_of(to * heads, heads), heads)],
                dst_ref=part_far.at[at],
                send_sem=p_send.at[at],
                recv_sem=p_recv.at[at],
                device_id=place(far_s if hop else me_s, to, me_d),
                device_id_type=MESH,
            )
            copy.start()
            part_copies.append(copy)

    upper = (
        lax.broadcasted_iota(jnp.int32, (tokens, tokens), 0)
        <= lax.broadcasted_iota(jnp.int32, (tokens, tokens), 1)
    )
    summing = upper.astype(jnp.float32)
    square = lax.broadcasted_iota(jnp.int32, (heads, heads), 0) == lax.broadcasted_iota(
        jnp.int32, (heads, heads), 1
    )

    def column(row):
        return jnp.sum(jnp.where(square, row, 0.0), axis=1, keepdims=True)

    bias = column(bias_ref[...])
    rate = jnp.exp(column(rate_ref[...]))
    spread_rows = lax.rem(lax.broadcasted_iota(jnp.int32, (2 * heads, heads * p_size), 0), heads)
    spread_at = lax.broadcasted_iota(jnp.int32, (2 * heads, heads * p_size), 1) // p_size
    spread = jnp.where(spread_rows == spread_at, 1.0, 0.0).astype(jnp.bfloat16)

    def widen(v):
        high, low = two_parts(v)
        return mm(jnp.concatenate([high, low], axis=0), spread, TN)

    for k in range(1, n_head):
        part_copies[2 * k - 1].wait_recv()
    preact = part[pl.ds(pl.multiple_of(me_h * heads, heads), heads), :] + bias
    for k in range(1, n_head):
        preact = preact + part_far[2 * k - 1]
    dt = softplus(preact)
    cum = exact_mm(-rate * dt, summing)
    total = cum[:, tokens - 1 :]
    cum_col = jnp.transpose(cum)
    dt_col = jnp.transpose(dt)
    dkt = jnp.zeros((tokens, tokens), jnp.float32)
    r_rows = []
    for h in range(heads):
        gap = cum[h : h + 1, :] - cum_col[:, h : h + 1]
        span = jnp.exp(jnp.where(upper, gap, -1e30))
        ke[h] = (kt * span).astype(jnp.bfloat16)
        step_here = dt_col[:, h : h + 1]
        f = mt[h] * span
        dkt = dkt + f * step_here
        prod = f * kt
        qcol[:, h : h + 1] = jnp.sum(prod, axis=1, keepdims=True)
        r_rows.append(jnp.sum(prod * step_here, axis=0, keepdims=True))
    r = jnp.concatenate(r_rows, axis=0)
    q = jnp.transpose(qcol[...])[:heads]

    first = me_s == 0
    for k in range(n_head):
        part_copies[2 * k].wait_recv()
    far_pre = bias
    for k in range(n_head):
        far_pre = far_pre + part_far[2 * k]
    far_dt = softplus(far_pre)
    far_cum = exact_mm(-rate * far_dt, summing)
    far_total = far_cum[:, tokens - 1 :]
    from_start = jnp.exp(cum)
    to_end = jnp.exp(total - cum)
    far_scale = jnp.where(first, jnp.exp(far_cum), jnp.exp(far_total - far_cum) * far_dt)
    near_scale = jnp.where(first, to_end * dt, from_start)
    far_wide = widen(far_scale)
    near_wide = widen(near_scale)
    raw_copies[0].wait_recv()
    far_rows = far_bc[...]
    near_rows = bc[me_s]
    states, carried, inputs = [], [], []
    w = jnp.zeros((heads, tokens), jnp.float32)
    for c, lanes in enumerate(chunks):
        raw_copies[c + 1].wait_recv()
        scaled = far_xg[:, lanes].astype(jnp.float32) * far_wide[:, lanes]
        states.append(mm(far_rows, scaled.astype(jnp.bfloat16), TN).astype(jnp.bfloat16))
        carried.append(mm(near_rows, states[c], NN))
        inputs.append(xg[me_s, :, lanes].astype(jnp.float32))
        high, low = two_parts(inputs[c] * carried[c])
        w = w + mm(spread[:heads, lanes], high, NT) + mm(spread[:heads, lanes], low, NT)

    v = to_end * w
    q = jnp.where(first, q + v, q)
    da = r - dt * q + jnp.where(first, 0.0, from_start * w)
    at_end = jnp.where(first, jnp.sum(dt * v, axis=1, keepdims=True), 0.0)
    lower = (
        lax.broadcasted_iota(jnp.int32, (tokens, tokens), 0)
        >= lax.broadcasted_iota(jnp.int32, (tokens, tokens), 1)
    ).astype(jnp.float32)
    grad_step = q - rate * (exact_mm(da, lower) + at_end)
    my_rows = pl.ds(pl.multiple_of(me_h * heads, heads), heads)
    gp_all[my_rows, :] = (grad_step * jax.nn.sigmoid(preact)).astype(jnp.bfloat16)
    gp_copies = []
    for k in range(1, n_head):
        copy = pltpu.make_async_remote_copy(
            src_ref=gp_all.at[my_rows],
            dst_ref=gp_all.at[my_rows],
            send_sem=g_send.at[k - 1],
            recv_sem=g_recv.at[k - 1],
            device_id=place(me_s, head_at(k), me_d),
            device_id_type=MESH,
        )
        copy.start()
        gp_copies.append(copy)

    dt_wide = widen(dt)
    flag = jnp.where(first, 1.0, 0.0)
    brought = jnp.concatenate(carried, axis=1)
    for j in range(heads // 2):
        lanes = slice(j * pair, (j + 1) * pair)
        gy_pair = xg[1, :, lanes]
        inner = jnp.where(left, mm(ke[2 * j], gy_pair, NN), mm(ke[2 * j + 1], gy_pair, NN))
        gx_ref[:, lanes] = (
            inner * dt_wide[:, lanes] + flag * near_wide[:, lanes] * brought[:, lanes]
        ).astype(jnp.bfloat16)
    extra = jnp.zeros_like(dkt)
    for c, lanes in enumerate(chunks):
        extra = extra + mm((inputs[c] * near_wide[:, lanes]).astype(jnp.bfloat16), states[c], NT)
    dk = dkt.astype(jnp.bfloat16)
    gb_ref[...] = (mm(dk, bc[1], NN) + flag * extra).astype(jnp.bfloat16)
    gc_ref[...] = (mm(dk, bc[0], TN) + (1.0 - flag) * extra).astype(jnp.bfloat16)

    for copy in gp_copies:
        copy.wait_recv()
    gw_send[...] = mm(gp_all[...], layer[...], NN).astype(jnp.bfloat16)
    gw_copies = []
    for cut in range(cuts):
        row = me_h * cuts + cut
        to_s, to_d = row // n_dp, lax.rem(row, n_dp)
        for k in range(n_head):
            to = head_at(k)
            at = cut * n_head + k
            block = gw_send.at[
                pl.ds(pl.multiple_of(to * heads, heads), heads),
                cut * rows_out : (cut + 1) * rows_out,
            ]
            copy = pltpu.make_async_remote_copy(
                src_ref=block,
                dst_ref=gw_recv.at[my_row],
                send_sem=d_send.at[at],
                recv_sem=d_recv.at[my_row],
                device_id=place(to_s, to, to_d),
                device_id_type=MESH,
            )
            if k:
                copy.start()
                gw_copies.append((copy, None))
            else:
                away = row != my_row
                pl.when(away)(copy.start)
                gw_copies.append((copy, away))

                @pl.when(jnp.logical_not(away))
                def _():
                    gw_recv[my_row] = block[...]

    gin = jnp.zeros((tokens, feats), jnp.float32)
    for j in range(n_head):
        rows = slice(j * heads, (j + 1) * heads)
        term = mm(gp_all[rows, :], w_all[rows, :], TN)
        gin = gin + term.astype(jnp.bfloat16).astype(jnp.float32)
    gin_ref[...] = gin.astype(jnp.bfloat16)

    def arrived(k):
        spot = lax.rem(my_row + k, share)
        return pltpu.make_async_remote_copy(
            src_ref=gw_recv.at[spot],
            dst_ref=gw_recv.at[spot],
            send_sem=d_send.at[0],
            recv_sem=d_recv.at[spot],
            device_id=place(far_s, me_h, me_d),
            device_id_type=MESH,
        )

    for k in range(1, share):
        arrived(k).wait_recv()
    pl.when(jnp.logical_not(mine))(arrived(0).wait_recv)
    gw = gw_recv[0].astype(jnp.float32)
    for k in range(1, share):
        gw = gw + gw_recv[k].astype(jnp.float32)
    gw_ref[...] = gw

    for copy in w_copies + raw_copies + part_copies + gp_copies:
        copy.wait_send()
    for copy, away in gw_copies:
        if away is None:
            copy.wait_send()
        else:
            pl.when(away)(copy.wait_send)


def write_out(*refs):
    sems = refs[-1]
    count = len(refs) // 2
    copies = [
        pltpu.make_async_copy(refs[i], refs[count + i], sems.at[i]) for i in range(count)
    ]
    for copy in copies:
        copy.start()
    for copy in copies:
        copy.wait()


def fused_body(
    mesh, layer_input, head_input, in_matrix, out_matrix, grad_output, step_weight, step_bias, decay_log
):
    n_seq, n_head, n_dp = (mesh.shape[a] for a in ("seq", "head", "dp"))
    tokens, feats = layer_input.shape[1:]
    width = head_input.shape[2]
    state_size = in_matrix.shape[2]
    heads = step_bias.shape[0]
    rows_out = step_weight.shape[0] // (n_seq * n_dp)
    share = n_seq * n_dp
    b16, f32 = jnp.bfloat16, jnp.float32
    dma = pltpu.SemaphoreType.DMA
    hbm = pl.BlockSpec(memory_space=pltpu.HBM)
    results = pl.pallas_call(
        functools.partial(mixer_kernel, (n_seq, n_head, n_dp, heads, width // heads)),
        out_shape=(
            pltpu.VMEM((tokens, width), b16),
            pltpu.VMEM((tokens, state_size), b16),
            pltpu.VMEM((tokens, state_size), b16),
            pltpu.VMEM((tokens, feats), b16),
            pltpu.VMEM((heads, rows_out), f32),
        ),
        in_specs=[hbm] * 8,
        out_specs=[pl.BlockSpec(memory_space=pltpu.VMEM)] * 5,
        scratch_shapes=[
            pltpu.VMEM((1, heads), f32),
            pltpu.VMEM((1, heads), f32),
            pltpu.VMEM((tokens, feats), b16),
            pltpu.VMEM((2, tokens, width), b16),
            pltpu.VMEM((2, tokens, state_size), b16),
            pltpu.VMEM((tokens, width), b16),
            pltpu.VMEM((tokens, state_size), b16),
            pltpu.VMEM((n_head * heads, feats), b16),
            pltpu.VMEM((n_head * heads, tokens), f32),
            pltpu.VMEM((2 * n_head - 1, heads, tokens), f32),
            pltpu.VMEM((heads, tokens, tokens), f32),
            pltpu.VMEM((heads, tokens, tokens), b16),
            pltpu.VMEM((tokens, tokens), f32),
            pltpu.VMEM((n_head * heads, tokens), b16),
            pltpu.VMEM((n_head * heads, feats), b16),
            pltpu.VMEM((share, heads, rows_out), b16),
            dma((8,)),
            dma((n_head - 1,)),
            dma((n_head - 1,)),
            dma((CHUNKS + 1,)),
            dma((CHUNKS + 1,)),
            dma((2 * n_head - 1,)),
            dma((2 * n_head - 1,)),
            dma((n_head - 1,)),
            dma((n_head - 1,)),
            dma((share,)),
            dma((share,)),
        ],
        compiler_params=pltpu.CompilerParams(
            collective_id=0, has_side_effects=True, vmem_limit_bytes=32 * 1024 * 1024
        ),
        name="mixer",
    )(
        *(
            pltpu.with_memory_space_constraint(a, pltpu.HBM)
            for a in (
                layer_input[0], head_input[0], in_matrix[0], out_matrix[0], grad_output[0],
                jnp.transpose(step_weight), step_bias[None], decay_log[None],
            )
        )
    )
    count = len(results)
    gx, gb, gc, gin, gw = pl.pallas_call(
        write_out,
        out_shape=tuple(jax.ShapeDtypeStruct(a.shape, a.dtype) for a in results),
        in_specs=[pl.BlockSpec(memory_space=pl.ANY)] * count,
        out_specs=[hbm] * count,
        scratch_shapes=[dma((count,))],
        name="write_out",
    )(*results)
    return gx[None], gb[None], gc[None], gin[None], jnp.transpose(gw)


def fits(mesh, args):
    n_seq, n_head, n_dp = (mesh.shape[a] for a in ("seq", "head", "dp"))
    tokens = args[0].shape[1] // n_seq
    return (
        n_seq == 2
        and n_head == G
        and tokens == BLOCK
        and (n_seq * n_dp) % n_head == 0
    )


def solution(mesh):
    in_specs = (
        P("dp", "seq", "head"),
        P("dp", "seq", "head"),
        P("dp", "seq", "head"),
        P("dp", "seq", "head"),
        P("dp", "seq", "head"),
        P(None, "head"),
        P("head"),
        P("head"),
    )
    out_specs = (
        P("dp", "seq", "head"),
        P("dp", "seq", "head"),
        P("dp", "seq", "head"),
        P("dp", "seq", "head"),
        P(("seq", "dp"), "head"),
    )

    def run(*args):
        here = functools.partial(fused_body, mesh) if fits(mesh, args) else body
        return jax.shard_map(
            here, mesh=mesh, in_specs=in_specs, out_specs=out_specs, check_vma=False
        )(*args)

    return run
```

```python
import functools

import jax
import jax.numpy as jnp
from jax import lax
from jax.experimental import pallas as pl
from jax.experimental.pallas import tpu as pltpu
from jax.sharding import PartitionSpec as P

H = 64
P_SIZE = 64
NSTATE = 128
G = 4
BLOCK = 128


PRECISION_LEVEL = lax.Precision.HIGHEST


def prefix(value, axis, join, neutral, backward):
    count = lax.axis_size(axis)
    place = lax.axis_index(axis)
    ahead = count - 1 - place if backward else place
    gathered = jax.tree.map(
        lambda a, kind: lax.all_gather(a.astype(kind), axis), value, (jnp.bfloat16, jnp.bfloat16)
    )
    state = jax.tree.map(lambda a, e: jnp.zeros_like(a) + jnp.asarray(e, a.dtype), value, neutral)

    def one(step, state):
        source = count - 1 - step if backward else step
        return join(
            state,
            jax.tree.map(
                lambda a, own: lax.dynamic_index_in_dim(a, source, 0, False).astype(own.dtype),
                gathered,
                value,
            ),
        )

    return lax.fori_loop(0, ahead, one, state)


def block_step(carry_state, inputs):
    input_block, b_block, c_block, step_block, decay_block = inputs
    cumulated = jnp.cumsum(decay_block, axis=-1)
    block_len = cumulated.shape[-1]
    lower_mask = jnp.arange(block_len)[:, None] >= jnp.arange(block_len)[None, :]
    decay_span = jnp.exp(
        jnp.where(lower_mask, cumulated[..., :, None] - cumulated[..., None, :], -1e30)
    )
    kernel = jnp.einsum("tgn,sgn->gts", c_block, b_block, precision=PRECISION_LEVEL)
    weight_values = kernel[:, None] * decay_span * step_block[..., None, :]
    within_block = jnp.einsum(
        "idwz,zidx->widx", weight_values, input_block, precision=PRECISION_LEVEL
    )
    carried = jnp.einsum("tgn,grnp->tgrp", c_block, carry_state, precision=PRECISION_LEVEL)
    output = within_block + jnp.moveaxis(jnp.exp(cumulated), -1, 0)[..., None] * carried
    totals = cumulated[..., -1]
    inflow = jnp.exp(totals[..., None] - cumulated) * step_block
    fresh_term = jnp.einsum(
        "grs,sgn,sgrp->grnp", inflow, b_block, input_block, precision=PRECISION_LEVEL
    )
    return (jnp.exp(totals)[..., None, None] * carry_state + fresh_term, output)


def segment(x_rows, b_rows, readout_rows, step_sizes, decays, start_state):
    length = x_rows.shape[0]
    blocks = length // BLOCK

    def split_rows(values):
        return values.reshape((blocks, BLOCK) + values.shape[1:])

    def split_last(values):
        return jnp.moveaxis(values.reshape(values.shape[:-1] + (blocks, BLOCK)), -2, 0)

    final_state, outputs = lax.scan(
        block_step,
        start_state,
        (
            split_rows(x_rows),
            split_rows(b_rows),
            split_rows(readout_rows),
            split_last(step_sizes),
            split_last(decays),
        ),
    )
    return (outputs.reshape(x_rows.shape), final_state)


def join_pairs(earlier, later):
    return (earlier[0] + later[0], jnp.exp(later[0])[..., None, None] * earlier[1] + later[1])


def body(
    layer_input, head_input, in_matrix, out_matrix, grad_output, step_weight, step_bias, decay_log
):
    tokens = head_input.shape[1]
    group_count = in_matrix.shape[2] // NSTATE
    ratio = H // G
    heads_here = group_count * ratio
    whole_input = lax.all_gather(layer_input, "head", axis=2, tiled=True)[0]
    preact = jnp.dot(whole_input, step_weight, preferred_element_type=jnp.float32) + step_bias
    step_sizes = jnp.transpose(jax.nn.softplus(preact)).reshape(group_count, ratio, tokens)
    rates = jnp.exp(decay_log).reshape(group_count, ratio)
    decays = -rates[..., None] * step_sizes
    x_rows = head_input[0].astype(jnp.float32).reshape(tokens, group_count, ratio, P_SIZE)
    b_rows = in_matrix[0].astype(jnp.float32).reshape(tokens, group_count, NSTATE)
    readout_rows = out_matrix[0].astype(jnp.float32).reshape(tokens, group_count, NSTATE)
    output_gradient = grad_output[0].astype(jnp.float32).reshape(tokens, group_count, ratio, P_SIZE)
    running_state = jnp.cumsum(decays, axis=-1)
    totals = running_state[..., -1]
    local_state = jnp.einsum(
        "grs,sgn,sgrp->grnp",
        jnp.exp(totals[..., None] - running_state) * step_sizes,
        b_rows,
        x_rows,
        precision=PRECISION_LEVEL,
    )
    local_grad = jnp.einsum(
        "vad,dvm,dvah->vamh",
        jnp.exp(running_state),
        readout_rows,
        output_gradient,
        precision=PRECISION_LEVEL,
    )
    neutral = (jnp.zeros_like(totals), jnp.zeros_like(local_state))
    incoming = prefix((totals, local_state), "seq", join_pairs, neutral, False)[1]
    outgoing = prefix((totals, local_grad), "seq", join_pairs, neutral, True)[1]

    def local_map(x_arg, b_arg, c_arg, step_arg):
        return segment(x_arg, b_arg, c_arg, step_arg, -rates[..., None] * step_arg, incoming)

    forward_out, pullback = jax.vjp(local_map, x_rows, b_rows, readout_rows, step_sizes)
    grad_x, grad_b, grad_c, grad_step = pullback((output_gradient, outgoing))
    grad_pre = (
        jnp.transpose(grad_step.reshape(heads_here, tokens)) * jax.nn.sigmoid(preact)
    ).astype(jnp.bfloat16)
    partial_terms = lax.dot_general(
        grad_pre, step_weight, (((1,), (1,)), ((), ())), preferred_element_type=jnp.float32
    )
    grad_input = lax.psum_scatter(
        partial_terms.astype(jnp.bfloat16), "head", scatter_dimension=1, tiled=True
    )
    seq_part = lax.psum_scatter(
        lax.dot_general(
            whole_input, grad_pre, (((0,), (0,)), ((), ())), preferred_element_type=jnp.float32
        ).astype(jnp.bfloat16),
        "seq",
        scatter_dimension=0,
        tiled=True,
    ).astype(jnp.float32)
    grad_weight = lax.psum_scatter(seq_part, "dp", scatter_dimension=0, tiled=True)
    return (
        grad_x.reshape(tokens, heads_here * P_SIZE).astype(jnp.bfloat16)[None],
        grad_b.reshape(tokens, group_count * NSTATE).astype(jnp.bfloat16)[None],
        grad_c.reshape(tokens, group_count * NSTATE).astype(jnp.bfloat16)[None],
        grad_input[None],
        grad_weight,
    )


MESH = pl.DeviceIdType.MESH
CHUNKS = 4
NT = (((1,), (1,)), ((), ()))
NN = (((1,), (0,)), ((), ()))
TN = (((0,), (0,)), ((), ()))


def mm(a, b, dims):
    return lax.dot_general(a, b, dims, preferred_element_type=jnp.float32)


def exact_mm(a, b):
    return lax.dot_general(
        a, b, NN, precision=lax.Precision.HIGHEST, preferred_element_type=jnp.float32
    )


def two_parts(v):
    high = v.astype(jnp.bfloat16)
    low = (v - high.astype(jnp.float32)).astype(jnp.bfloat16)
    return high, low


def softplus(v):
    return jnp.maximum(v, 0.0) + jnp.log1p(jnp.exp(-jnp.abs(v)))


def mixer_kernel(
    sizes,
    layer_hbm, x_hbm, b_hbm, c_hbm, gy_hbm, w_hbm, bias_hbm, rate_hbm,
    gx_ref, gb_ref, gc_ref, gin_ref, gw_ref,
    bias_ref, rate_ref, layer, xg, bc, far_xg, far_bc, w_all, part, part_far, mt, ke, qcol, gp_all, gw_send, gw_recv,
    load_sem, w_send, w_recv, raw_send, raw_recv, p_send, p_recv, g_send, g_recv, d_send, d_recv,
):
    n_seq, n_head, n_dp, heads, p_size = sizes
    tokens, feats = layer.shape
    me_s, me_h, me_d = lax.axis_index("seq"), lax.axis_index("head"), lax.axis_index("dp")
    far_s = 1 - me_s
    rows_out = gw_ref.shape[1]
    cuts = feats // rows_out
    share = n_seq * n_dp

    def head_at(k):
        return lax.rem(me_h + k, n_head)

    def place(s, h, d):
        return {"seq": s, "head": h, "dp": d}

    loads = [
        pltpu.make_async_copy(x_hbm, xg.at[0], load_sem.at[0]),
        pltpu.make_async_copy(gy_hbm, xg.at[1], load_sem.at[1]),
        pltpu.make_async_copy(b_hbm, bc.at[0], load_sem.at[2]),
        pltpu.make_async_copy(c_hbm, bc.at[1], load_sem.at[3]),
        pltpu.make_async_copy(layer_hbm, layer, load_sem.at[4]),
        pltpu.make_async_copy(
            w_hbm.at[:, pl.ds(pl.multiple_of(me_h * feats, feats), feats)],
            w_all.at[pl.ds(pl.multiple_of(me_h * heads, heads), heads)],
            load_sem.at[5],
        ),
        pltpu.make_async_copy(bias_hbm, bias_ref, load_sem.at[6]),
        pltpu.make_async_copy(rate_hbm, rate_ref, load_sem.at[7]),
    ]
    for load in loads:
        load.start()

    barrier = pltpu.get_barrier_semaphore()
    my_row = me_s * n_dp + me_d
    source_h = my_row // cuts
    for k in range(n_head):
        if k:
            pl.semaphore_signal(
                barrier, inc=1, device_id=place(me_s, head_at(k), me_d), device_id_type=MESH
            )
        pl.semaphore_signal(
            barrier, inc=1, device_id=place(far_s, head_at(k), me_d), device_id_type=MESH
        )
    mine = source_h == me_h
    for k in range(share):
        spot = lax.rem(my_row + k, share)

        def greet():
            pl.semaphore_signal(
                barrier,
                inc=1,
                device_id=place(spot // n_dp, source_h, lax.rem(spot, n_dp)),
                device_id_type=MESH,
            )

        if k:
            greet()
        else:
            pl.when(jnp.logical_not(mine))(greet)
    pl.semaphore_wait(barrier, 2 * n_head - 1 + share - jnp.where(mine, 1, 0))

    w_copies = []
    for k in range(1, n_head):
        to = head_at(k)
        copy = pltpu.make_async_remote_copy(
            src_ref=w_hbm.at[:, pl.ds(pl.multiple_of(to * feats, feats), feats)],
            dst_ref=w_all.at[pl.ds(pl.multiple_of(me_h * heads, heads), heads)],
            send_sem=w_send.at[k - 1],
            recv_sem=w_recv.at[k - 1],
            device_id=place(me_s, to, me_d),
            device_id_type=MESH,
        )
        copy.start()
        w_copies.append(copy)

    for load in loads[:4]:
        load.wait()
    raw_copies = []
    width = far_xg.shape[1] // CHUNKS
    chunks = [slice(c * width, (c + 1) * width) for c in range(CHUNKS)]
    near_refs = [bc.at[me_s]] + [xg.at[me_s, :, lanes] for lanes in chunks]
    far_refs = [far_bc] + [far_xg.at[:, lanes] for lanes in chunks]
    for at in range(CHUNKS + 1):
        copy = pltpu.make_async_remote_copy(
            src_ref=near_refs[at],
            dst_ref=far_refs[at],
            send_sem=raw_send.at[at],
            recv_sem=raw_recv.at[at],
            device_id=place(far_s, me_h, me_d),
            device_id_type=MESH,
        )
        copy.start()
        raw_copies.append(copy)

    pair = 2 * p_size
    left = lax.broadcasted_iota(jnp.int32, (tokens, pair), 1) < p_size
    kt = mm(bc[0], bc[1], NT)
    zero_pair = jnp.zeros((tokens, pair), jnp.bfloat16)
    for j in range(heads // 2):
        lanes = slice(j * pair, (j + 1) * pair)
        x_pair, gy_pair = xg[0, :, lanes], xg[1, :, lanes]
        mt[2 * j] = mm(jnp.where(left, x_pair, zero_pair), gy_pair, NT)
        mt[2 * j + 1] = mm(jnp.where(left, zero_pair, x_pair), gy_pair, NT)

    for load in loads[4:]:
        load.wait()
    for copy in w_copies:
        copy.wait_recv()
    part[...] = mm(w_all[...], layer[...], NT)
    part_copies = []
    for k in range(n_head):
        to = head_at(k)
        for hop in range(2):
            if k == 0 and hop == 0:
                continue
            at = 2 * k + hop - 1
            copy = pltpu.make_async_remote_copy(
                src_ref=part.at[pl.ds(pl.multiple_of(to * heads, heads), heads)],
                dst_ref=part_far.at[at],
                send_sem=p_send.at[at],
                recv_sem=p_recv.at[at],
                device_id=place(far_s if hop else me_s, to, me_d),
                device_id_type=MESH,
            )
            copy.start()
            part_copies.append(copy)

    upper = (
        lax.broadcasted_iota(jnp.int32, (tokens, tokens), 0)
        <= lax.broadcasted_iota(jnp.int32, (tokens, tokens), 1)
    )
    summing = upper.astype(jnp.float32)
    square = lax.broadcasted_iota(jnp.int32, (heads, heads), 0) == lax.broadcasted_iota(
        jnp.int32, (heads, heads), 1
    )

    def column(row):
        return jnp.sum(jnp.where(square, row, 0.0), axis=1, keepdims=True)

    bias = column(bias_ref[...])
    rate = jnp.exp(column(rate_ref[...]))
    spread_rows = lax.rem(lax.broadcasted_iota(jnp.int32, (2 * heads, heads * p_size), 0), heads)
    spread_at = lax.broadcasted_iota(jnp.int32, (2 * heads, heads * p_size), 1) // p_size
    spread = jnp.where(spread_rows == spread_at, 1.0, 0.0).astype(jnp.bfloat16)

    def widen(v):
        high, low = two_parts(v)
        return mm(jnp.concatenate([high, low], axis=0), spread, TN)

    for k in range(1, n_head):
        part_copies[2 * k - 1].wait_recv()
    preact = part[pl.ds(pl.multiple_of(me_h * heads, heads), heads), :] + bias
    for k in range(1, n_head):
        preact = preact + part_far[2 * k - 1]
    dt = softplus(preact)
    cum = exact_mm(-rate * dt, summing)
    total = cum[:, tokens - 1 :]
    cum_col = jnp.transpose(cum)
    dt_col = jnp.transpose(dt)
    dkt = jnp.zeros((tokens, tokens), jnp.float32)
    r_rows = []
    for h in range(heads):
        gap = cum[h : h + 1, :] - cum_col[:, h : h + 1]
        span = jnp.exp(jnp.where(upper, gap, -1e30))
        ke[h] = (kt * span).astype(jnp.bfloat16)
        step_here = dt_col[:, h : h + 1]
        f = mt[h] * span
        dkt = dkt + f * step_here
        prod = f * kt
        qcol[:, h : h + 1] = jnp.sum(prod, axis=1, keepdims=True)
        r_rows.append(jnp.sum(prod * step_here, axis=0, keepdims=True))
    r = jnp.concatenate(r_rows, axis=0)
    q = jnp.transpose(qcol[...])[:heads]

    first = me_s == 0
    for k in range(n_head):
        part_copies[2 * k].wait_recv()
    far_pre = bias
    for k in range(n_head):
        far_pre = far_pre + part_far[2 * k]
    far_dt = softplus(far_pre)
    far_cum = exact_mm(-rate * far_dt, summing)
    far_total = far_cum[:, tokens - 1 :]
    from_start = jnp.exp(cum)
    to_end = jnp.exp(total - cum)
    far_scale = jnp.where(first, jnp.exp(far_cum), jnp.exp(far_total - far_cum) * far_dt)
    near_scale = jnp.where(first, to_end * dt, from_start)
    far_wide = widen(far_scale)
    near_wide = widen(near_scale)
    raw_copies[0].wait_recv()
    far_rows = far_bc[...]
    near_rows = bc[me_s]
    states, carried, inputs = [], [], []
    w = jnp.zeros((heads, tokens), jnp.float32)
    for c, lanes in enumerate(chunks):
        raw_copies[c + 1].wait_recv()
        scaled = far_xg[:, lanes].astype(jnp.float32) * far_wide[:, lanes]
        states.append(mm(far_rows, scaled.astype(jnp.bfloat16), TN).astype(jnp.bfloat16))
        carried.append(mm(near_rows, states[c], NN))
        inputs.append(xg[me_s, :, lanes].astype(jnp.float32))
        high, low = two_parts(inputs[c] * carried[c])
        w = w + mm(spread[:heads, lanes], high, NT) + mm(spread[:heads, lanes], low, NT)

    v = to_end * w
    q = jnp.where(first, q + v, q)
    da = r - dt * q + jnp.where(first, 0.0, from_start * w)
    at_end = jnp.where(first, jnp.sum(dt * v, axis=1, keepdims=True), 0.0)
    lower = (
        lax.broadcasted_iota(jnp.int32, (tokens, tokens), 0)
        >= lax.broadcasted_iota(jnp.int32, (tokens, tokens), 1)
    ).astype(jnp.float32)
    grad_step = q - rate * (exact_mm(da, lower) + at_end)
    my_rows = pl.ds(pl.multiple_of(me_h * heads, heads), heads)
    gp_all[my_rows, :] = (grad_step * jax.nn.sigmoid(preact)).astype(jnp.bfloat16)
    gp_copies = []
    for k in range(1, n_head):
        copy = pltpu.make_async_remote_copy(
            src_ref=gp_all.at[my_rows],
            dst_ref=gp_all.at[my_rows],
            send_sem=g_send.at[k - 1],
            recv_sem=g_recv.at[k - 1],
            device_id=place(me_s, head_at(k), me_d),
            device_id_type=MESH,
        )
        copy.start()
        gp_copies.append(copy)

    dt_wide = widen(dt)
    flag = jnp.where(first, 1.0, 0.0)
    brought = jnp.concatenate(carried, axis=1)
    for j in range(heads // 2):
        lanes = slice(j * pair, (j + 1) * pair)
        gy_pair = xg[1, :, lanes]
        inner = jnp.where(left, mm(ke[2 * j], gy_pair, NN), mm(ke[2 * j + 1], gy_pair, NN))
        gx_ref[:, lanes] = (
            inner * dt_wide[:, lanes] + flag * near_wide[:, lanes] * brought[:, lanes]
        ).astype(jnp.bfloat16)
    extra = jnp.zeros_like(dkt)
    for c, lanes in enumerate(chunks):
        extra = extra + mm((inputs[c] * near_wide[:, lanes]).astype(jnp.bfloat16), states[c], NT)
    dk = dkt.astype(jnp.bfloat16)
    gb_ref[...] = (mm(dk, bc[1], NN) + flag * extra).astype(jnp.bfloat16)
    gc_ref[...] = (mm(dk, bc[0], TN) + (1.0 - flag) * extra).astype(jnp.bfloat16)

    for copy in gp_copies:
        copy.wait_recv()
    gw_send[...] = mm(gp_all[...], layer[...], NN).astype(jnp.bfloat16)
    gw_copies = []
    for cut in range(cuts):
        row = me_h * cuts + cut
        to_s, to_d = row // n_dp, lax.rem(row, n_dp)
        for k in range(n_head):
            to = head_at(k)
            at = cut * n_head + k
            block = gw_send.at[
                pl.ds(pl.multiple_of(to * heads, heads), heads),
                cut * rows_out : (cut + 1) * rows_out,
            ]
            copy = pltpu.make_async_remote_copy(
                src_ref=block,
                dst_ref=gw_recv.at[my_row],
                send_sem=d_send.at[at],
                recv_sem=d_recv.at[my_row],
                device_id=place(to_s, to, to_d),
                device_id_type=MESH,
            )
            if k:
                copy.start()
                gw_copies.append((copy, None))
            else:
                away = row != my_row
                pl.when(away)(copy.start)
                gw_copies.append((copy, away))

                @pl.when(jnp.logical_not(away))
                def _():
                    gw_recv[my_row] = block[...]

    gin = jnp.zeros((tokens, feats), jnp.float32)
    for j in range(n_head):
        rows = slice(j * heads, (j + 1) * heads)
        term = mm(gp_all[rows, :], w_all[rows, :], TN)
        gin = gin + term.astype(jnp.bfloat16).astype(jnp.float32)
    gin_ref[...] = gin.astype(jnp.bfloat16)

    def arrived(k):
        spot = lax.rem(my_row + k, share)
        return pltpu.make_async_remote_copy(
            src_ref=gw_recv.at[spot],
            dst_ref=gw_recv.at[spot],
            send_sem=d_send.at[0],
            recv_sem=d_recv.at[spot],
            device_id=place(far_s, me_h, me_d),
            device_id_type=MESH,
        )

    for k in range(1, share):
        arrived(k).wait_recv()
    pl.when(jnp.logical_not(mine))(arrived(0).wait_recv)
    gw = gw_recv[0].astype(jnp.float32)
    for k in range(1, share):
        gw = gw + gw_recv[k].astype(jnp.float32)
    gw_ref[...] = gw

    for copy in w_copies + raw_copies + part_copies + gp_copies:
        copy.wait_send()
    for copy, away in gw_copies:
        if away is None:
            copy.wait_send()
        else:
            pl.when(away)(copy.wait_send)


def write_out(*refs):
    sems = refs[-1]
    count = len(refs) // 2
    copies = [
        pltpu.make_async_copy(refs[i], refs[count + i], sems.at[i]) for i in range(count)
    ]
    for copy in copies:
        copy.start()
    for copy in copies:
        copy.wait()


def fused_body(
    mesh, layer_input, head_input, in_matrix, out_matrix, grad_output, step_weight, step_bias, decay_log
):
    n_seq, n_head, n_dp = (mesh.shape[a] for a in ("seq", "head", "dp"))
    tokens, feats = layer_input.shape[1:]
    width = head_input.shape[2]
    state_size = in_matrix.shape[2]
    heads = step_bias.shape[0]
    rows_out = step_weight.shape[0] // (n_seq * n_dp)
    share = n_seq * n_dp
    b16, f32 = jnp.bfloat16, jnp.float32
    dma = pltpu.SemaphoreType.DMA
    hbm = pl.BlockSpec(memory_space=pltpu.HBM)
    results = pl.pallas_call(
        functools.partial(mixer_kernel, (n_seq, n_head, n_dp, heads, width // heads)),
        out_shape=(
            pltpu.VMEM((tokens, width), b16),
            pltpu.VMEM((tokens, state_size), b16),
            pltpu.VMEM((tokens, state_size), b16),
            pltpu.VMEM((tokens, feats), b16),
            pltpu.VMEM((heads, rows_out), f32),
        ),
        in_specs=[hbm] * 8,
        out_specs=[pl.BlockSpec(memory_space=pltpu.VMEM)] * 5,
        scratch_shapes=[
            pltpu.VMEM((1, heads), f32),
            pltpu.VMEM((1, heads), f32),
            pltpu.VMEM((tokens, feats), b16),
            pltpu.VMEM((2, tokens, width), b16),
            pltpu.VMEM((2, tokens, state_size), b16),
            pltpu.VMEM((tokens, width), b16),
            pltpu.VMEM((tokens, state_size), b16),
            pltpu.VMEM((n_head * heads, feats), b16),
            pltpu.VMEM((n_head * heads, tokens), f32),
            pltpu.VMEM((2 * n_head - 1, heads, tokens), f32),
            pltpu.VMEM((heads, tokens, tokens), f32),
            pltpu.VMEM((heads, tokens, tokens), b16),
            pltpu.VMEM((tokens, tokens), f32),
            pltpu.VMEM((n_head * heads, tokens), b16),
            pltpu.VMEM((n_head * heads, feats), b16),
            pltpu.VMEM((share, heads, rows_out), b16),
            dma((8,)),
            dma((n_head - 1,)),
            dma((n_head - 1,)),
            dma((CHUNKS + 1,)),
            dma((CHUNKS + 1,)),
            dma((2 * n_head - 1,)),
            dma((2 * n_head - 1,)),
            dma((n_head - 1,)),
            dma((n_head - 1,)),
            dma((share,)),
            dma((share,)),
        ],
        compiler_params=pltpu.CompilerParams(
            collective_id=0, has_side_effects=True, vmem_limit_bytes=32 * 1024 * 1024
        ),
        name="mixer",
    )(
        *(
            pltpu.with_memory_space_constraint(a, pltpu.HBM)
            for a in (
                layer_input[0], head_input[0], in_matrix[0], out_matrix[0], grad_output[0],
                jnp.transpose(step_weight), step_bias[None], decay_log[None],
            )
        )
    )
    count = len(results)
    gx, gb, gc, gin, gw = pl.pallas_call(
        write_out,
        out_shape=tuple(jax.ShapeDtypeStruct(a.shape, a.dtype) for a in results),
        in_specs=[pl.BlockSpec(memory_space=pl.ANY)] * count,
        out_specs=[hbm] * count,
        scratch_shapes=[dma((count,))],
        compiler_params=pltpu.CompilerParams(vmem_limit_bytes=4 * 1024 * 1024),
        name="write_out",
    )(*(pltpu.with_memory_space_constraint(a, pltpu.VMEM) for a in results))
    return gx[None], gb[None], gc[None], gin[None], jnp.transpose(gw)


def fits(mesh, args):
    n_seq, n_head, n_dp = (mesh.shape[a] for a in ("seq", "head", "dp"))
    tokens = args[0].shape[1] // n_seq
    return (
        n_seq == 2
        and n_head == G
        and tokens == BLOCK
        and (n_seq * n_dp) % n_head == 0
    )


def solution(mesh):
    in_specs = (
        P("dp", "seq", "head"),
        P("dp", "seq", "head"),
        P("dp", "seq", "head"),
        P("dp", "seq", "head"),
        P("dp", "seq", "head"),
        P(None, "head"),
        P("head"),
        P("head"),
    )
    out_specs = (
        P("dp", "seq", "head"),
        P("dp", "seq", "head"),
        P("dp", "seq", "head"),
        P("dp", "seq", "head"),
        P(("seq", "dp"), "head"),
    )

    def run(*args):
        here = functools.partial(fused_body, mesh) if fits(mesh, args) else body
        return jax.shard_map(
            here, mesh=mesh, in_specs=in_specs, out_specs=out_specs, check_vma=False
        )(*args)

    return run
```

```python
import functools

import jax
import jax.numpy as jnp
from jax import lax
from jax.experimental import pallas as pl
from jax.experimental.pallas import tpu as pltpu
from jax.sharding import PartitionSpec as P

H = 64
P_SIZE = 64
NSTATE = 128
G = 4
BLOCK = 128


PRECISION_LEVEL = lax.Precision.HIGHEST


def prefix(value, axis, join, neutral, backward):
    count = lax.axis_size(axis)
    place = lax.axis_index(axis)
    ahead = count - 1 - place if backward else place
    gathered = jax.tree.map(
        lambda a, kind: lax.all_gather(a.astype(kind), axis), value, (jnp.bfloat16, jnp.bfloat16)
    )
    state = jax.tree.map(lambda a, e: jnp.zeros_like(a) + jnp.asarray(e, a.dtype), value, neutral)

    def one(step, state):
        source = count - 1 - step if backward else step
        return join(
            state,
            jax.tree.map(
                lambda a, own: lax.dynamic_index_in_dim(a, source, 0, False).astype(own.dtype),
                gathered,
                value,
            ),
        )

    return lax.fori_loop(0, ahead, one, state)


def block_step(carry_state, inputs):
    input_block, b_block, c_block, step_block, decay_block = inputs
    cumulated = jnp.cumsum(decay_block, axis=-1)
    block_len = cumulated.shape[-1]
    lower_mask = jnp.arange(block_len)[:, None] >= jnp.arange(block_len)[None, :]
    decay_span = jnp.exp(
        jnp.where(lower_mask, cumulated[..., :, None] - cumulated[..., None, :], -1e30)
    )
    kernel = jnp.einsum("tgn,sgn->gts", c_block, b_block, precision=PRECISION_LEVEL)
    weight_values = kernel[:, None] * decay_span * step_block[..., None, :]
    within_block = jnp.einsum(
        "idwz,zidx->widx", weight_values, input_block, precision=PRECISION_LEVEL
    )
    carried = jnp.einsum("tgn,grnp->tgrp", c_block, carry_state, precision=PRECISION_LEVEL)
    output = within_block + jnp.moveaxis(jnp.exp(cumulated), -1, 0)[..., None] * carried
    totals = cumulated[..., -1]
    inflow = jnp.exp(totals[..., None] - cumulated) * step_block
    fresh_term = jnp.einsum(
        "grs,sgn,sgrp->grnp", inflow, b_block, input_block, precision=PRECISION_LEVEL
    )
    return (jnp.exp(totals)[..., None, None] * carry_state + fresh_term, output)


def segment(x_rows, b_rows, readout_rows, step_sizes, decays, start_state):
    length = x_rows.shape[0]
    blocks = length // BLOCK

    def split_rows(values):
        return values.reshape((blocks, BLOCK) + values.shape[1:])

    def split_last(values):
        return jnp.moveaxis(values.reshape(values.shape[:-1] + (blocks, BLOCK)), -2, 0)

    final_state, outputs = lax.scan(
        block_step,
        start_state,
        (
            split_rows(x_rows),
            split_rows(b_rows),
            split_rows(readout_rows),
            split_last(step_sizes),
            split_last(decays),
        ),
    )
    return (outputs.reshape(x_rows.shape), final_state)


def join_pairs(earlier, later):
    return (earlier[0] + later[0], jnp.exp(later[0])[..., None, None] * earlier[1] + later[1])


def body(
    layer_input, head_input, in_matrix, out_matrix, grad_output, step_weight, step_bias, decay_log
):
    tokens = head_input.shape[1]
    group_count = in_matrix.shape[2] // NSTATE
    ratio = H // G
    heads_here = group_count * ratio
    whole_input = lax.all_gather(layer_input, "head", axis=2, tiled=True)[0]
    preact = jnp.dot(whole_input, step_weight, preferred_element_type=jnp.float32) + step_bias
    step_sizes = jnp.transpose(jax.nn.softplus(preact)).reshape(group_count, ratio, tokens)
    rates = jnp.exp(decay_log).reshape(group_count, ratio)
    decays = -rates[..., None] * step_sizes
    x_rows = head_input[0].astype(jnp.float32).reshape(tokens, group_count, ratio, P_SIZE)
    b_rows = in_matrix[0].astype(jnp.float32).reshape(tokens, group_count, NSTATE)
    readout_rows = out_matrix[0].astype(jnp.float32).reshape(tokens, group_count, NSTATE)
    output_gradient = grad_output[0].astype(jnp.float32).reshape(tokens, group_count, ratio, P_SIZE)
    running_state = jnp.cumsum(decays, axis=-1)
    totals = running_state[..., -1]
    local_state = jnp.einsum(
        "grs,sgn,sgrp->grnp",
        jnp.exp(totals[..., None] - running_state) * step_sizes,
        b_rows,
        x_rows,
        precision=PRECISION_LEVEL,
    )
    local_grad = jnp.einsum(
        "vad,dvm,dvah->vamh",
        jnp.exp(running_state),
        readout_rows,
        output_gradient,
        precision=PRECISION_LEVEL,
    )
    neutral = (jnp.zeros_like(totals), jnp.zeros_like(local_state))
    incoming = prefix((totals, local_state), "seq", join_pairs, neutral, False)[1]
    outgoing = prefix((totals, local_grad), "seq", join_pairs, neutral, True)[1]

    def local_map(x_arg, b_arg, c_arg, step_arg):
        return segment(x_arg, b_arg, c_arg, step_arg, -rates[..., None] * step_arg, incoming)

    forward_out, pullback = jax.vjp(local_map, x_rows, b_rows, readout_rows, step_sizes)
    grad_x, grad_b, grad_c, grad_step = pullback((output_gradient, outgoing))
    grad_pre = (
        jnp.transpose(grad_step.reshape(heads_here, tokens)) * jax.nn.sigmoid(preact)
    ).astype(jnp.bfloat16)
    partial_terms = lax.dot_general(
        grad_pre, step_weight, (((1,), (1,)), ((), ())), preferred_element_type=jnp.float32
    )
    grad_input = lax.psum_scatter(
        partial_terms.astype(jnp.bfloat16), "head", scatter_dimension=1, tiled=True
    )
    seq_part = lax.psum_scatter(
        lax.dot_general(
            whole_input, grad_pre, (((0,), (0,)), ((), ())), preferred_element_type=jnp.float32
        ).astype(jnp.bfloat16),
        "seq",
        scatter_dimension=0,
        tiled=True,
    ).astype(jnp.float32)
    grad_weight = lax.psum_scatter(seq_part, "dp", scatter_dimension=0, tiled=True)
    return (
        grad_x.reshape(tokens, heads_here * P_SIZE).astype(jnp.bfloat16)[None],
        grad_b.reshape(tokens, group_count * NSTATE).astype(jnp.bfloat16)[None],
        grad_c.reshape(tokens, group_count * NSTATE).astype(jnp.bfloat16)[None],
        grad_input[None],
        grad_weight,
    )


MESH = pl.DeviceIdType.MESH
CHUNKS = 4
NT = (((1,), (1,)), ((), ()))
NN = (((1,), (0,)), ((), ()))
TN = (((0,), (0,)), ((), ()))


def mm(a, b, dims):
    return lax.dot_general(a, b, dims, preferred_element_type=jnp.float32)


def exact_mm(a, b):
    return lax.dot_general(
        a, b, NN, precision=lax.Precision.HIGHEST, preferred_element_type=jnp.float32
    )


def two_parts(v):
    high = v.astype(jnp.bfloat16)
    low = (v - high.astype(jnp.float32)).astype(jnp.bfloat16)
    return high, low


def softplus(v):
    return jnp.maximum(v, 0.0) + jnp.log1p(jnp.exp(-jnp.abs(v)))


def mixer_kernel(
    sizes,
    layer_hbm, x_hbm, b_hbm, c_hbm, gy_hbm, w_hbm, bias_hbm, rate_hbm,
    gx_ref, gb_ref, gc_ref, gin_ref, gw_ref,
    bias_ref, rate_ref, layer, xg, bc, far_xg, far_bc, w_all, part, part_far, mt, ke, qcol, gp_all, gw_send, gw_recv,
    load_sem, w_send, w_recv, raw_send, raw_recv, p_send, p_recv, g_send, g_recv, d_send, d_recv,
):
    n_seq, n_head, n_dp, heads, p_size = sizes
    tokens, feats = layer.shape
    me_s, me_h, me_d = lax.axis_index("seq"), lax.axis_index("head"), lax.axis_index("dp")
    far_s = 1 - me_s
    rows_out = gw_ref.shape[1]
    cuts = feats // rows_out
    share = n_seq * n_dp

    def head_at(k):
        return lax.rem(me_h + k, n_head)

    def place(s, h, d):
        return {"seq": s, "head": h, "dp": d}

    loads = [
        pltpu.make_async_copy(x_hbm, xg.at[0], load_sem.at[0]),
        pltpu.make_async_copy(gy_hbm, xg.at[1], load_sem.at[1]),
        pltpu.make_async_copy(b_hbm, bc.at[0], load_sem.at[2]),
        pltpu.make_async_copy(c_hbm, bc.at[1], load_sem.at[3]),
        pltpu.make_async_copy(layer_hbm, layer, load_sem.at[4]),
        pltpu.make_async_copy(
            w_hbm.at[:, pl.ds(pl.multiple_of(me_h * feats, feats), feats)],
            w_all.at[pl.ds(pl.multiple_of(me_h * heads, heads), heads)],
            load_sem.at[5],
        ),
        pltpu.make_async_copy(bias_hbm, bias_ref, load_sem.at[6]),
        pltpu.make_async_copy(rate_hbm, rate_ref, load_sem.at[7]),
    ]
    for load in loads:
        load.start()

    barrier = pltpu.get_barrier_semaphore()
    my_row = me_s * n_dp + me_d
    source_h = my_row // cuts
    for k in range(n_head):
        if k:
            pl.semaphore_signal(
                barrier, inc=1, device_id=place(me_s, head_at(k), me_d), device_id_type=MESH
            )
        pl.semaphore_signal(
            barrier, inc=1, device_id=place(far_s, head_at(k), me_d), device_id_type=MESH
        )
    mine = source_h == me_h
    for k in range(share):
        spot = lax.rem(my_row + k, share)

        def greet():
            pl.semaphore_signal(
                barrier,
                inc=1,
                device_id=place(spot // n_dp, source_h, lax.rem(spot, n_dp)),
                device_id_type=MESH,
            )

        if k:
            greet()
        else:
            pl.when(jnp.logical_not(mine))(greet)
    pl.semaphore_wait(barrier, 2 * n_head - 1 + share - jnp.where(mine, 1, 0))

    w_copies = []
    for k in range(1, n_head):
        to = head_at(k)
        copy = pltpu.make_async_remote_copy(
            src_ref=w_hbm.at[:, pl.ds(pl.multiple_of(to * feats, feats), feats)],
            dst_ref=w_all.at[pl.ds(pl.multiple_of(me_h * heads, heads), heads)],
            send_sem=w_send.at[k - 1],
            recv_sem=w_recv.at[k - 1],
            device_id=place(me_s, to, me_d),
            device_id_type=MESH,
        )
        copy.start()
        w_copies.append(copy)

    for load in loads[:4]:
        load.wait()
    raw_copies = []
    width = far_xg.shape[1] // CHUNKS
    chunks = [slice(c * width, (c + 1) * width) for c in range(CHUNKS)]
    near_refs = [bc.at[me_s]] + [xg.at[me_s, :, lanes] for lanes in chunks]
    far_refs = [far_bc] + [far_xg.at[:, lanes] for lanes in chunks]
    for at in range(CHUNKS + 1):
        copy = pltpu.make_async_remote_copy(
            src_ref=near_refs[at],
            dst_ref=far_refs[at],
            send_sem=raw_send.at[at],
            recv_sem=raw_recv.at[at],
            device_id=place(far_s, me_h, me_d),
            device_id_type=MESH,
        )
        raw_copies.append(copy)
    for copy in raw_copies[: 1 + CHUNKS // 2]:
        copy.start()

    pair = 2 * p_size
    left = lax.broadcasted_iota(jnp.int32, (tokens, pair), 1) < p_size
    kt = mm(bc[0], bc[1], NT)
    zero_pair = jnp.zeros((tokens, pair), jnp.bfloat16)
    for j in range(heads // 2):
        lanes = slice(j * pair, (j + 1) * pair)
        x_pair, gy_pair = xg[0, :, lanes], xg[1, :, lanes]
        mt[2 * j] = mm(jnp.where(left, x_pair, zero_pair), gy_pair, NT)
        mt[2 * j + 1] = mm(jnp.where(left, zero_pair, x_pair), gy_pair, NT)

    for load in loads[4:]:
        load.wait()
    for copy in w_copies:
        copy.wait_recv()
    part[...] = mm(w_all[...], layer[...], NT)
    part_copies = []
    for k in range(n_head):
        to = head_at(k)
        for hop in range(2):
            if k == 0 and hop == 0:
                continue
            at = 2 * k + hop - 1
            copy = pltpu.make_async_remote_copy(
                src_ref=part.at[pl.ds(pl.multiple_of(to * heads, heads), heads)],
                dst_ref=part_far.at[at],
                send_sem=p_send.at[at],
                recv_sem=p_recv.at[at],
                device_id=place(far_s if hop else me_s, to, me_d),
                device_id_type=MESH,
            )
            copy.start()
            part_copies.append(copy)
    for copy in raw_copies[1 + CHUNKS // 2 :]:
        copy.start()

    upper = (
        lax.broadcasted_iota(jnp.int32, (tokens, tokens), 0)
        <= lax.broadcasted_iota(jnp.int32, (tokens, tokens), 1)
    )
    summing = upper.astype(jnp.float32)
    square = lax.broadcasted_iota(jnp.int32, (heads, heads), 0) == lax.broadcasted_iota(
        jnp.int32, (heads, heads), 1
    )

    def column(row):
        return jnp.sum(jnp.where(square, row, 0.0), axis=1, keepdims=True)

    bias = column(bias_ref[...])
    rate = jnp.exp(column(rate_ref[...]))
    spread_rows = lax.rem(lax.broadcasted_iota(jnp.int32, (2 * heads, heads * p_size), 0), heads)
    spread_at = lax.broadcasted_iota(jnp.int32, (2 * heads, heads * p_size), 1) // p_size
    spread = jnp.where(spread_rows == spread_at, 1.0, 0.0).astype(jnp.bfloat16)

    def widen(v):
        high, low = two_parts(v)
        return mm(jnp.concatenate([high, low], axis=0), spread, TN)

    for k in range(1, n_head):
        part_copies[2 * k - 1].wait_recv()
    preact = part[pl.ds(pl.multiple_of(me_h * heads, heads), heads), :] + bias
    for k in range(1, n_head):
        preact = preact + part_far[2 * k - 1]
    dt = softplus(preact)
    cum = exact_mm(-rate * dt, summing)
    total = cum[:, tokens - 1 :]
    cum_col = jnp.transpose(cum)
    dt_col = jnp.transpose(dt)
    dkt = jnp.zeros((tokens, tokens), jnp.float32)
    r_rows = []
    for h in range(heads):
        if h == heads // 2:
            first = me_s == 0
            for k in range(n_head):
                part_copies[2 * k].wait_recv()
            far_pre = bias
            for k in range(n_head):
                far_pre = far_pre + part_far[2 * k]
            far_dt = softplus(far_pre)
            far_cum = exact_mm(-rate * far_dt, summing)
            far_total = far_cum[:, tokens - 1 :]
            from_start = jnp.exp(cum)
            to_end = jnp.exp(total - cum)
            far_scale = jnp.where(first, jnp.exp(far_cum), jnp.exp(far_total - far_cum) * far_dt)
            near_scale = jnp.where(first, to_end * dt, from_start)
            far_wide = widen(far_scale)
            near_wide = widen(near_scale)
        gap = cum[h : h + 1, :] - cum_col[:, h : h + 1]
        span = jnp.exp(jnp.where(upper, gap, -1e30))
        ke[h] = (kt * span).astype(jnp.bfloat16)
        step_here = dt_col[:, h : h + 1]
        f = mt[h] * span
        dkt = dkt + f * step_here
        prod = f * kt
        qcol[:, h : h + 1] = jnp.sum(prod, axis=1, keepdims=True)
        r_rows.append(jnp.sum(prod * step_here, axis=0, keepdims=True))
    r = jnp.concatenate(r_rows, axis=0)
    q = jnp.transpose(qcol[...])[:heads]

    for copy in raw_copies:
        copy.wait_recv()
    far_rows = far_bc[...]
    near_rows = bc[me_s]
    states, carried, inputs = [], [], []
    w = jnp.zeros((heads, tokens), jnp.float32)
    for c, lanes in enumerate(chunks):
        scaled = far_xg[:, lanes].astype(jnp.float32) * far_wide[:, lanes]
        states.append(mm(far_rows, scaled.astype(jnp.bfloat16), TN).astype(jnp.bfloat16))
        carried.append(mm(near_rows, states[c], NN))
        inputs.append(xg[me_s, :, lanes].astype(jnp.float32))
        high, low = two_parts(inputs[c] * carried[c])
        w = w + mm(spread[:heads, lanes], high, NT) + mm(spread[:heads, lanes], low, NT)

    v = to_end * w
    q = jnp.where(first, q + v, q)
    da = r - dt * q + jnp.where(first, 0.0, from_start * w)
    at_end = jnp.where(first, jnp.sum(dt * v, axis=1, keepdims=True), 0.0)
    lower = (
        lax.broadcasted_iota(jnp.int32, (tokens, tokens), 0)
        >= lax.broadcasted_iota(jnp.int32, (tokens, tokens), 1)
    ).astype(jnp.float32)
    grad_step = q - rate * (exact_mm(da, lower) + at_end)
    my_rows = pl.ds(pl.multiple_of(me_h * heads, heads), heads)
    gp_all[my_rows, :] = (grad_step * jax.nn.sigmoid(preact)).astype(jnp.bfloat16)
    gp_copies = []
    for k in range(1, n_head):
        copy = pltpu.make_async_remote_copy(
            src_ref=gp_all.at[my_rows],
            dst_ref=gp_all.at[my_rows],
            send_sem=g_send.at[k - 1],
            recv_sem=g_recv.at[k - 1],
            device_id=place(me_s, head_at(k), me_d),
            device_id_type=MESH,
        )
        copy.start()
        gp_copies.append(copy)

    dt_wide = widen(dt)
    flag = jnp.where(first, 1.0, 0.0)
    brought = jnp.concatenate(carried, axis=1)
    for j in range(heads // 2):
        lanes = slice(j * pair, (j + 1) * pair)
        gy_pair = xg[1, :, lanes]
        inner = jnp.where(left, mm(ke[2 * j], gy_pair, NN), mm(ke[2 * j + 1], gy_pair, NN))
        gx_ref[:, lanes] = (
            inner * dt_wide[:, lanes] + flag * near_wide[:, lanes] * brought[:, lanes]
        ).astype(jnp.bfloat16)

    for copy in gp_copies:
        copy.wait_recv()
    gw_send[...] = mm(gp_all[...], layer[...], NN).astype(jnp.bfloat16)
    gw_copies = []
    for cut in range(cuts):
        row = me_h * cuts + cut
        to_s, to_d = row // n_dp, lax.rem(row, n_dp)
        for k in range(n_head):
            to = head_at(k)
            at = cut * n_head + k
            block = gw_send.at[
                pl.ds(pl.multiple_of(to * heads, heads), heads),
                cut * rows_out : (cut + 1) * rows_out,
            ]
            copy = pltpu.make_async_remote_copy(
                src_ref=block,
                dst_ref=gw_recv.at[my_row],
                send_sem=d_send.at[at],
                recv_sem=d_recv.at[my_row],
                device_id=place(to_s, to, to_d),
                device_id_type=MESH,
            )
            if k:
                copy.start()
                gw_copies.append((copy, None))
            else:
                away = row != my_row
                pl.when(away)(copy.start)
                gw_copies.append((copy, away))

                @pl.when(jnp.logical_not(away))
                def _():
                    gw_recv[my_row] = block[...]

    extra = jnp.zeros_like(dkt)
    for c, lanes in enumerate(chunks):
        extra = extra + mm((inputs[c] * near_wide[:, lanes]).astype(jnp.bfloat16), states[c], NT)
    dk = dkt.astype(jnp.bfloat16)
    gb_ref[...] = (mm(dk, bc[1], NN) + flag * extra).astype(jnp.bfloat16)
    gc_ref[...] = (mm(dk, bc[0], TN) + (1.0 - flag) * extra).astype(jnp.bfloat16)

    gin = jnp.zeros((tokens, feats), jnp.float32)
    for j in range(n_head):
        rows = slice(j * heads, (j + 1) * heads)
        term = mm(gp_all[rows, :], w_all[rows, :], TN)
        gin = gin + term.astype(jnp.bfloat16).astype(jnp.float32)
    gin_ref[...] = gin.astype(jnp.bfloat16)

    def arrived(k):
        spot = lax.rem(my_row + k, share)
        return pltpu.make_async_remote_copy(
            src_ref=gw_recv.at[spot],
            dst_ref=gw_recv.at[spot],
            send_sem=d_send.at[0],
            recv_sem=d_recv.at[spot],
            device_id=place(far_s, me_h, me_d),
            device_id_type=MESH,
        )

    for k in range(1, share):
        arrived(k).wait_recv()
    pl.when(jnp.logical_not(mine))(arrived(0).wait_recv)
    gw = gw_recv[0].astype(jnp.float32)
    for k in range(1, share):
        gw = gw + gw_recv[k].astype(jnp.float32)
    gw_ref[...] = gw

    for copy in w_copies + raw_copies + part_copies + gp_copies:
        copy.wait_send()
    for copy, away in gw_copies:
        if away is None:
            copy.wait_send()
        else:
            pl.when(away)(copy.wait_send)


def write_out(*refs):
    sems = refs[-1]
    count = len(refs) // 2
    copies = [
        pltpu.make_async_copy(refs[i], refs[count + i], sems.at[i]) for i in range(count)
    ]
    for copy in copies:
        copy.start()
    for copy in copies:
        copy.wait()


def fused_body(
    mesh, layer_input, head_input, in_matrix, out_matrix, grad_output, step_weight, step_bias, decay_log
):
    n_seq, n_head, n_dp = (mesh.shape[a] for a in ("seq", "head", "dp"))
    tokens, feats = layer_input.shape[1:]
    width = head_input.shape[2]
    state_size = in_matrix.shape[2]
    heads = step_bias.shape[0]
    rows_out = step_weight.shape[0] // (n_seq * n_dp)
    share = n_seq * n_dp
    b16, f32 = jnp.bfloat16, jnp.float32
    dma = pltpu.SemaphoreType.DMA
    hbm = pl.BlockSpec(memory_space=pltpu.HBM)
    results = pl.pallas_call(
        functools.partial(mixer_kernel, (n_seq, n_head, n_dp, heads, width // heads)),
        out_shape=(
            pltpu.VMEM((tokens, width), b16),
            pltpu.VMEM((tokens, state_size), b16),
            pltpu.VMEM((tokens, state_size), b16),
            pltpu.VMEM((tokens, feats), b16),
            pltpu.VMEM((heads, rows_out), f32),
        ),
        in_specs=[hbm] * 8,
        out_specs=[pl.BlockSpec(memory_space=pltpu.VMEM)] * 5,
        scratch_shapes=[
            pltpu.VMEM((1, heads), f32),
            pltpu.VMEM((1, heads), f32),
            pltpu.VMEM((tokens, feats), b16),
            pltpu.VMEM((2, tokens, width), b16),
            pltpu.VMEM((2, tokens, state_size), b16),
            pltpu.VMEM((tokens, width), b16),
            pltpu.VMEM((tokens, state_size), b16),
            pltpu.VMEM((n_head * heads, feats), b16),
            pltpu.VMEM((n_head * heads, tokens), f32),
            pltpu.VMEM((2 * n_head - 1, heads, tokens), f32),
            pltpu.VMEM((heads, tokens, tokens), f32),
            pltpu.VMEM((heads, tokens, tokens), b16),
            pltpu.VMEM((tokens, tokens), f32),
            pltpu.VMEM((n_head * heads, tokens), b16),
            pltpu.VMEM((n_head * heads, feats), b16),
            pltpu.VMEM((share, heads, rows_out), b16),
            dma((8,)),
            dma((n_head - 1,)),
            dma((n_head - 1,)),
            dma((CHUNKS + 1,)),
            dma((CHUNKS + 1,)),
            dma((2 * n_head - 1,)),
            dma((2 * n_head - 1,)),
            dma((n_head - 1,)),
            dma((n_head - 1,)),
            dma((share,)),
            dma((share,)),
        ],
        compiler_params=pltpu.CompilerParams(
            collective_id=0, has_side_effects=True, vmem_limit_bytes=32 * 1024 * 1024
        ),
        name="mixer",
    )(
        *(
            pltpu.with_memory_space_constraint(a, pltpu.HBM)
            for a in (
                layer_input[0], head_input[0], in_matrix[0], out_matrix[0], grad_output[0],
                jnp.transpose(step_weight), step_bias[None], decay_log[None],
            )
        )
    )
    count = len(results)
    gx, gb, gc, gin, gw = pl.pallas_call(
        write_out,
        out_shape=tuple(jax.ShapeDtypeStruct(a.shape, a.dtype) for a in results),
        in_specs=[pl.BlockSpec(memory_space=pl.ANY)] * count,
        out_specs=[hbm] * count,
        scratch_shapes=[dma((count,))],
        compiler_params=pltpu.CompilerParams(vmem_limit_bytes=4 * 1024 * 1024),
        name="write_out",
    )(*(pltpu.with_memory_space_constraint(a, pltpu.VMEM) for a in results))
    return gx[None], gb[None], gc[None], gin[None], jnp.transpose(gw)


def fits(mesh, args):
    n_seq, n_head, n_dp = (mesh.shape[a] for a in ("seq", "head", "dp"))
    tokens = args[0].shape[1] // n_seq
    return (
        n_seq == 2
        and n_head == G
        and tokens == BLOCK
        and (n_seq * n_dp) % n_head == 0
    )


def solution(mesh):
    in_specs = (
        P("dp", "seq", "head"),
        P("dp", "seq", "head"),
        P("dp", "seq", "head"),
        P("dp", "seq", "head"),
        P("dp", "seq", "head"),
        P(None, "head"),
        P("head"),
        P("head"),
    )
    out_specs = (
        P("dp", "seq", "head"),
        P("dp", "seq", "head"),
        P("dp", "seq", "head"),
        P("dp", "seq", "head"),
        P(("seq", "dp"), "head"),
    )

    def run(*args):
        here = functools.partial(fused_body, mesh) if fits(mesh, args) else body
        return jax.shard_map(
            here, mesh=mesh, in_specs=in_specs, out_specs=out_specs, check_vma=False
        )(*args)

    return run
```

```python
import functools

import jax
import jax.numpy as jnp
from jax import lax
from jax.experimental import pallas as pl
from jax.experimental.pallas import tpu as pltpu
from jax.sharding import PartitionSpec as P

H = 64
P_SIZE = 64
NSTATE = 128
G = 4
BLOCK = 128


PRECISION_LEVEL = lax.Precision.HIGHEST


def prefix(value, axis, join, neutral, backward):
    count = lax.axis_size(axis)
    place = lax.axis_index(axis)
    ahead = count - 1 - place if backward else place
    gathered = jax.tree.map(
        lambda a, kind: lax.all_gather(a.astype(kind), axis), value, (jnp.bfloat16, jnp.bfloat16)
    )
    state = jax.tree.map(lambda a, e: jnp.zeros_like(a) + jnp.asarray(e, a.dtype), value, neutral)

    def one(step, state):
        source = count - 1 - step if backward else step
        return join(
            state,
            jax.tree.map(
                lambda a, own: lax.dynamic_index_in_dim(a, source, 0, False).astype(own.dtype),
                gathered,
                value,
            ),
        )

    return lax.fori_loop(0, ahead, one, state)


def block_step(carry_state, inputs):
    input_block, b_block, c_block, step_block, decay_block = inputs
    cumulated = jnp.cumsum(decay_block, axis=-1)
    block_len = cumulated.shape[-1]
    lower_mask = jnp.arange(block_len)[:, None] >= jnp.arange(block_len)[None, :]
    decay_span = jnp.exp(
        jnp.where(lower_mask, cumulated[..., :, None] - cumulated[..., None, :], -1e30)
    )
    kernel = jnp.einsum("tgn,sgn->gts", c_block, b_block, precision=PRECISION_LEVEL)
    weight_values = kernel[:, None] * decay_span * step_block[..., None, :]
    within_block = jnp.einsum(
        "idwz,zidx->widx", weight_values, input_block, precision=PRECISION_LEVEL
    )
    carried = jnp.einsum("tgn,grnp->tgrp", c_block, carry_state, precision=PRECISION_LEVEL)
    output = within_block + jnp.moveaxis(jnp.exp(cumulated), -1, 0)[..., None] * carried
    totals = cumulated[..., -1]
    inflow = jnp.exp(totals[..., None] - cumulated) * step_block
    fresh_term = jnp.einsum(
        "grs,sgn,sgrp->grnp", inflow, b_block, input_block, precision=PRECISION_LEVEL
    )
    return (jnp.exp(totals)[..., None, None] * carry_state + fresh_term, output)


def segment(x_rows, b_rows, readout_rows, step_sizes, decays, start_state):
    length = x_rows.shape[0]
    blocks = length // BLOCK

    def split_rows(values):
        return values.reshape((blocks, BLOCK) + values.shape[1:])

    def split_last(values):
        return jnp.moveaxis(values.reshape(values.shape[:-1] + (blocks, BLOCK)), -2, 0)

    final_state, outputs = lax.scan(
        block_step,
        start_state,
        (
            split_rows(x_rows),
            split_rows(b_rows),
            split_rows(readout_rows),
            split_last(step_sizes),
            split_last(decays),
        ),
    )
    return (outputs.reshape(x_rows.shape), final_state)


def join_pairs(earlier, later):
    return (earlier[0] + later[0], jnp.exp(later[0])[..., None, None] * earlier[1] + later[1])


def body(
    layer_input, head_input, in_matrix, out_matrix, grad_output, step_weight, step_bias, decay_log
):
    tokens = head_input.shape[1]
    group_count = in_matrix.shape[2] // NSTATE
    ratio = H // G
    heads_here = group_count * ratio
    whole_input = lax.all_gather(layer_input, "head", axis=2, tiled=True)[0]
    preact = jnp.dot(whole_input, step_weight, preferred_element_type=jnp.float32) + step_bias
    step_sizes = jnp.transpose(jax.nn.softplus(preact)).reshape(group_count, ratio, tokens)
    rates = jnp.exp(decay_log).reshape(group_count, ratio)
    decays = -rates[..., None] * step_sizes
    x_rows = head_input[0].astype(jnp.float32).reshape(tokens, group_count, ratio, P_SIZE)
    b_rows = in_matrix[0].astype(jnp.float32).reshape(tokens, group_count, NSTATE)
    readout_rows = out_matrix[0].astype(jnp.float32).reshape(tokens, group_count, NSTATE)
    output_gradient = grad_output[0].astype(jnp.float32).reshape(tokens, group_count, ratio, P_SIZE)
    running_state = jnp.cumsum(decays, axis=-1)
    totals = running_state[..., -1]
    local_state = jnp.einsum(
        "grs,sgn,sgrp->grnp",
        jnp.exp(totals[..., None] - running_state) * step_sizes,
        b_rows,
        x_rows,
        precision=PRECISION_LEVEL,
    )
    local_grad = jnp.einsum(
        "vad,dvm,dvah->vamh",
        jnp.exp(running_state),
        readout_rows,
        output_gradient,
        precision=PRECISION_LEVEL,
    )
    neutral = (jnp.zeros_like(totals), jnp.zeros_like(local_state))
    incoming = prefix((totals, local_state), "seq", join_pairs, neutral, False)[1]
    outgoing = prefix((totals, local_grad), "seq", join_pairs, neutral, True)[1]

    def local_map(x_arg, b_arg, c_arg, step_arg):
        return segment(x_arg, b_arg, c_arg, step_arg, -rates[..., None] * step_arg, incoming)

    forward_out, pullback = jax.vjp(local_map, x_rows, b_rows, readout_rows, step_sizes)
    grad_x, grad_b, grad_c, grad_step = pullback((output_gradient, outgoing))
    grad_pre = (
        jnp.transpose(grad_step.reshape(heads_here, tokens)) * jax.nn.sigmoid(preact)
    ).astype(jnp.bfloat16)
    partial_terms = lax.dot_general(
        grad_pre, step_weight, (((1,), (1,)), ((), ())), preferred_element_type=jnp.float32
    )
    grad_input = lax.psum_scatter(
        partial_terms.astype(jnp.bfloat16), "head", scatter_dimension=1, tiled=True
    )
    seq_part = lax.psum_scatter(
        lax.dot_general(
            whole_input, grad_pre, (((0,), (0,)), ((), ())), preferred_element_type=jnp.float32
        ).astype(jnp.bfloat16),
        "seq",
        scatter_dimension=0,
        tiled=True,
    ).astype(jnp.float32)
    grad_weight = lax.psum_scatter(seq_part, "dp", scatter_dimension=0, tiled=True)
    return (
        grad_x.reshape(tokens, heads_here * P_SIZE).astype(jnp.bfloat16)[None],
        grad_b.reshape(tokens, group_count * NSTATE).astype(jnp.bfloat16)[None],
        grad_c.reshape(tokens, group_count * NSTATE).astype(jnp.bfloat16)[None],
        grad_input[None],
        grad_weight,
    )


MESH = pl.DeviceIdType.MESH
CHUNKS = 4
NT = (((1,), (1,)), ((), ()))
NN = (((1,), (0,)), ((), ()))
TN = (((0,), (0,)), ((), ()))


def mm(a, b, dims):
    return lax.dot_general(a, b, dims, preferred_element_type=jnp.float32)


def exact_mm(a, ones):
    count = a.shape[0]
    parts = []
    for _ in range(3):
        parts.append(a.astype(jnp.bfloat16))
        a = a - parts[-1].astype(jnp.float32)
    sums = mm(jnp.concatenate(parts, axis=0), ones, NN)
    return sums[:count] + (sums[count : 2 * count] + sums[2 * count :])


def two_parts(v):
    high = v.astype(jnp.bfloat16)
    low = (v - high.astype(jnp.float32)).astype(jnp.bfloat16)
    return high, low


def softplus(v):
    return jnp.maximum(v, 0.0) + jnp.log1p(jnp.exp(-jnp.abs(v)))


def mixer_kernel(
    sizes,
    layer_hbm, x_hbm, b_hbm, c_hbm, gy_hbm, w_hbm, bias_hbm, rate_hbm,
    gx_ref, gb_ref, gc_ref, gin_ref, gw_ref,
    bias_ref, rate_ref, layer, xg, bc, far_xg, far_bc, w_all, part, part_far, mt, ke, qcol, gp_all, gw_send, gw_recv,
    load_sem, w_send, w_recv, raw_send, raw_recv, p_send, p_recv, g_send, g_recv, d_send, d_recv,
):
    n_seq, n_head, n_dp, heads, p_size = sizes
    tokens, feats = layer.shape
    me_s, me_h, me_d = lax.axis_index("seq"), lax.axis_index("head"), lax.axis_index("dp")
    far_s = 1 - me_s
    rows_out = gw_ref.shape[1]
    cuts = feats // rows_out
    share = n_seq * n_dp

    def head_at(k):
        return lax.rem(me_h + k, n_head)

    def place(s, h, d):
        return {"seq": s, "head": h, "dp": d}

    loads = [
        pltpu.make_async_copy(x_hbm, xg.at[0], load_sem.at[0]),
        pltpu.make_async_copy(gy_hbm, xg.at[1], load_sem.at[1]),
        pltpu.make_async_copy(b_hbm, bc.at[0], load_sem.at[2]),
        pltpu.make_async_copy(c_hbm, bc.at[1], load_sem.at[3]),
        pltpu.make_async_copy(layer_hbm, layer, load_sem.at[4]),
        pltpu.make_async_copy(
            w_hbm.at[:, pl.ds(pl.multiple_of(me_h * feats, feats), feats)],
            w_all.at[pl.ds(pl.multiple_of(me_h * heads, heads), heads)],
            load_sem.at[5],
        ),
        pltpu.make_async_copy(bias_hbm, bias_ref, load_sem.at[6]),
        pltpu.make_async_copy(rate_hbm, rate_ref, load_sem.at[7]),
    ]

    barrier = pltpu.get_barrier_semaphore()
    my_row = me_s * n_dp + me_d
    source_h = my_row // cuts
    for k in range(n_head):
        if k:
            pl.semaphore_signal(
                barrier, inc=1, device_id=place(me_s, head_at(k), me_d), device_id_type=MESH
            )
        pl.semaphore_signal(
            barrier, inc=1, device_id=place(far_s, head_at(k), me_d), device_id_type=MESH
        )
    mine = source_h == me_h
    for k in range(share):
        spot = lax.rem(my_row + k, share)

        def greet():
            pl.semaphore_signal(
                barrier,
                inc=1,
                device_id=place(spot // n_dp, source_h, lax.rem(spot, n_dp)),
                device_id_type=MESH,
            )

        if k:
            greet()
        else:
            pl.when(jnp.logical_not(mine))(greet)
    for load in loads:
        load.start()
    pl.semaphore_wait(barrier, 2 * n_head - 1 + share - jnp.where(mine, 1, 0))

    w_copies = []
    for k in range(1, n_head):
        to = head_at(k)
        copy = pltpu.make_async_remote_copy(
            src_ref=w_hbm.at[:, pl.ds(pl.multiple_of(to * feats, feats), feats)],
            dst_ref=w_all.at[pl.ds(pl.multiple_of(me_h * heads, heads), heads)],
            send_sem=w_send.at[k - 1],
            recv_sem=w_recv.at[k - 1],
            device_id=place(me_s, to, me_d),
            device_id_type=MESH,
        )
        copy.start()
        w_copies.append(copy)

    for load in loads[:4]:
        load.wait()
    raw_copies = []
    width = far_xg.shape[1] // CHUNKS
    chunks = [slice(c * width, (c + 1) * width) for c in range(CHUNKS)]
    near_refs = [bc.at[me_s]] + [xg.at[me_s, :, lanes] for lanes in chunks]
    far_refs = [far_bc] + [far_xg.at[:, lanes] for lanes in chunks]
    for at in range(CHUNKS + 1):
        copy = pltpu.make_async_remote_copy(
            src_ref=near_refs[at],
            dst_ref=far_refs[at],
            send_sem=raw_send.at[at],
            recv_sem=raw_recv.at[at],
            device_id=place(far_s, me_h, me_d),
            device_id_type=MESH,
        )
        raw_copies.append(copy)
    for copy in raw_copies[: 1 + CHUNKS // 2]:
        copy.start()

    pair = 2 * p_size
    left = lax.broadcasted_iota(jnp.int32, (tokens, pair), 1) < p_size
    kt = mm(bc[0], bc[1], NT)
    zero_pair = jnp.zeros((tokens, pair), jnp.bfloat16)
    for j in range(heads // 2):
        lanes = slice(j * pair, (j + 1) * pair)
        x_pair, gy_pair = xg[0, :, lanes], xg[1, :, lanes]
        mt[2 * j] = mm(jnp.where(left, x_pair, zero_pair), gy_pair, NT)
        mt[2 * j + 1] = mm(jnp.where(left, zero_pair, x_pair), gy_pair, NT)

    upper = (
        lax.broadcasted_iota(jnp.int32, (tokens, tokens), 0)
        <= lax.broadcasted_iota(jnp.int32, (tokens, tokens), 1)
    )
    summing = jnp.where(upper, 1.0, 0.0).astype(jnp.bfloat16)
    lower = jnp.where(
        lax.broadcasted_iota(jnp.int32, (tokens, tokens), 0)
        >= lax.broadcasted_iota(jnp.int32, (tokens, tokens), 1),
        1.0,
        0.0,
    ).astype(jnp.bfloat16)
    square = lax.broadcasted_iota(jnp.int32, (heads, heads), 0) == lax.broadcasted_iota(
        jnp.int32, (heads, heads), 1
    )

    def column(row):
        return jnp.sum(jnp.where(square, row, 0.0), axis=1, keepdims=True)

    spread_rows = lax.rem(lax.broadcasted_iota(jnp.int32, (2 * heads, heads * p_size), 0), heads)
    spread_at = lax.broadcasted_iota(jnp.int32, (2 * heads, heads * p_size), 1) // p_size
    spread = jnp.where(spread_rows == spread_at, 1.0, 0.0).astype(jnp.bfloat16)

    def widen(v):
        high, low = two_parts(v)
        return mm(jnp.concatenate([high, low], axis=0), spread, TN)

    for load in loads[4:]:
        load.wait()
    bias = column(bias_ref[...])
    rate = jnp.exp(column(rate_ref[...]))
    for copy in w_copies:
        copy.wait_recv()
    part[...] = mm(w_all[...], layer[...], NT)
    part_copies = {}
    for hop in range(2):
        for k in range(1 - hop, n_head):
            to = head_at(k)
            at = 2 * k + hop - 1
            copy = pltpu.make_async_remote_copy(
                src_ref=part.at[pl.ds(pl.multiple_of(to * heads, heads), heads)],
                dst_ref=part_far.at[at],
                send_sem=p_send.at[at],
                recv_sem=p_recv.at[at],
                device_id=place(far_s if hop else me_s, to, me_d),
                device_id_type=MESH,
            )
            copy.start()
            part_copies[at] = copy
    for copy in raw_copies[1 + CHUNKS // 2 :]:
        copy.start()

    for k in range(1, n_head):
        part_copies[2 * k - 1].wait_recv()
    preact = part[pl.ds(pl.multiple_of(me_h * heads, heads), heads), :] + bias
    for k in range(1, n_head):
        preact = preact + part_far[2 * k - 1]
    dt = softplus(preact)
    cum = exact_mm(-rate * dt, summing)
    total = cum[:, tokens - 1 :]
    cum_col = jnp.transpose(cum)
    dt_col = jnp.transpose(dt)
    dkt = jnp.zeros((tokens, tokens), jnp.float32)
    r_rows = []
    for h in range(heads):
        if h == heads // 2:
            first = me_s == 0
            for k in range(n_head):
                part_copies[2 * k].wait_recv()
            far_pre = bias
            for k in range(n_head):
                far_pre = far_pre + part_far[2 * k]
            far_dt = softplus(far_pre)
            far_cum = exact_mm(-rate * far_dt, summing)
            far_total = far_cum[:, tokens - 1 :]
            from_start = jnp.exp(cum)
            to_end = jnp.exp(total - cum)
            far_scale = jnp.where(first, jnp.exp(far_cum), jnp.exp(far_total - far_cum) * far_dt)
            near_scale = jnp.where(first, to_end * dt, from_start)
            far_wide = widen(far_scale)
            near_wide = widen(near_scale)
        gap = cum[h : h + 1, :] - cum_col[:, h : h + 1]
        span = jnp.exp(jnp.where(upper, gap, -1e30))
        ke[h] = (kt * span).astype(jnp.bfloat16)
        step_here = dt_col[:, h : h + 1]
        f = mt[h] * span
        dkt = dkt + f * step_here
        prod = f * kt
        qcol[:, h : h + 1] = jnp.sum(prod, axis=1, keepdims=True)
        r_rows.append(jnp.sum(prod * step_here, axis=0, keepdims=True))
    r = jnp.concatenate(r_rows, axis=0)
    q = jnp.transpose(qcol[...])[:heads]

    for copy in raw_copies:
        copy.wait_recv()
    far_rows = far_bc[...]
    near_rows = bc[me_s]
    states, carried, inputs = [], [], []
    w = jnp.zeros((heads, tokens), jnp.float32)
    for c, lanes in enumerate(chunks):
        scaled = far_xg[:, lanes].astype(jnp.float32) * far_wide[:, lanes]
        states.append(mm(far_rows, scaled.astype(jnp.bfloat16), TN).astype(jnp.bfloat16))
        carried.append(mm(near_rows, states[c], NN))
        inputs.append(xg[me_s, :, lanes].astype(jnp.float32))
        high, low = two_parts(inputs[c] * carried[c])
        w = w + mm(spread[:heads, lanes], high, NT) + mm(spread[:heads, lanes], low, NT)

    v = to_end * w
    q = jnp.where(first, q + v, q)
    da = r - dt * q + jnp.where(first, 0.0, from_start * w)
    at_end = jnp.where(first, jnp.sum(dt * v, axis=1, keepdims=True), 0.0)
    grad_step = q - rate * (exact_mm(da, lower) + at_end)
    my_rows = pl.ds(pl.multiple_of(me_h * heads, heads), heads)
    gp_all[my_rows, :] = (grad_step * jax.nn.sigmoid(preact)).astype(jnp.bfloat16)
    gp_copies = []
    for k in range(1, n_head):
        copy = pltpu.make_async_remote_copy(
            src_ref=gp_all.at[my_rows],
            dst_ref=gp_all.at[my_rows],
            send_sem=g_send.at[k - 1],
            recv_sem=g_recv.at[k - 1],
            device_id=place(me_s, head_at(k), me_d),
            device_id_type=MESH,
        )
        copy.start()
        gp_copies.append(copy)

    dt_wide = widen(dt)
    flag = jnp.where(first, 1.0, 0.0)
    brought = jnp.concatenate(carried, axis=1)
    for j in range(heads // 2):
        lanes = slice(j * pair, (j + 1) * pair)
        gy_pair = xg[1, :, lanes]
        inner = jnp.where(left, mm(ke[2 * j], gy_pair, NN), mm(ke[2 * j + 1], gy_pair, NN))
        gx_ref[:, lanes] = (
            inner * dt_wide[:, lanes] + flag * near_wide[:, lanes] * brought[:, lanes]
        ).astype(jnp.bfloat16)

    for copy in gp_copies:
        copy.wait_recv()
    gw_send[...] = mm(gp_all[...], layer[...], NN).astype(jnp.bfloat16)
    gw_copies = []
    for cut in range(cuts):
        row = me_h * cuts + cut
        to_s, to_d = row // n_dp, lax.rem(row, n_dp)
        for k in range(n_head):
            to = head_at(k)
            at = cut * n_head + k
            block = gw_send.at[
                pl.ds(pl.multiple_of(to * heads, heads), heads),
                cut * rows_out : (cut + 1) * rows_out,
            ]
            copy = pltpu.make_async_remote_copy(
                src_ref=block,
                dst_ref=gw_recv.at[my_row],
                send_sem=d_send.at[at],
                recv_sem=d_recv.at[my_row],
                device_id=place(to_s, to, to_d),
                device_id_type=MESH,
            )
            if k:
                copy.start()
                gw_copies.append((copy, None))
            else:
                away = row != my_row
                pl.when(away)(copy.start)
                gw_copies.append((copy, away))

                @pl.when(jnp.logical_not(away))
                def _():
                    gw_recv[my_row] = block[...]

    extra = jnp.zeros_like(dkt)
    for c, lanes in enumerate(chunks):
        extra = extra + mm((inputs[c] * near_wide[:, lanes]).astype(jnp.bfloat16), states[c], NT)
    dk = dkt.astype(jnp.bfloat16)
    gb_ref[...] = (mm(dk, bc[1], NN) + flag * extra).astype(jnp.bfloat16)
    gc_ref[...] = (mm(dk, bc[0], TN) + (1.0 - flag) * extra).astype(jnp.bfloat16)

    gin = jnp.zeros((tokens, feats), jnp.float32)
    for j in range(n_head):
        rows = slice(j * heads, (j + 1) * heads)
        term = mm(gp_all[rows, :], w_all[rows, :], TN)
        gin = gin + term.astype(jnp.bfloat16).astype(jnp.float32)
    gin_ref[...] = gin.astype(jnp.bfloat16)

    def arrived(k):
        spot = lax.rem(my_row + k, share)
        return pltpu.make_async_remote_copy(
            src_ref=gw_recv.at[spot],
            dst_ref=gw_recv.at[spot],
            send_sem=d_send.at[0],
            recv_sem=d_recv.at[spot],
            device_id=place(far_s, me_h, me_d),
            device_id_type=MESH,
        )

    for k in range(1, share):
        arrived(k).wait_recv()
    pl.when(jnp.logical_not(mine))(arrived(0).wait_recv)
    gw = gw_recv[0].astype(jnp.float32)
    for k in range(1, share):
        gw = gw + gw_recv[k].astype(jnp.float32)
    gw_ref[...] = gw

    for copy in w_copies + raw_copies + list(part_copies.values()) + gp_copies:
        copy.wait_send()
    for copy, away in gw_copies:
        if away is None:
            copy.wait_send()
        else:
            pl.when(away)(copy.wait_send)


def write_out(*refs):
    sems = refs[-1]
    count = len(refs) // 2
    copies = [
        pltpu.make_async_copy(refs[i], refs[count + i], sems.at[i]) for i in range(count)
    ]
    for copy in copies:
        copy.start()
    for copy in copies:
        copy.wait()


def fused_body(
    mesh, layer_input, head_input, in_matrix, out_matrix, grad_output, step_weight, step_bias, decay_log
):
    n_seq, n_head, n_dp = (mesh.shape[a] for a in ("seq", "head", "dp"))
    tokens, feats = layer_input.shape[1:]
    width = head_input.shape[2]
    state_size = in_matrix.shape[2]
    heads = step_bias.shape[0]
    rows_out = step_weight.shape[0] // (n_seq * n_dp)
    share = n_seq * n_dp
    b16, f32 = jnp.bfloat16, jnp.float32
    dma = pltpu.SemaphoreType.DMA
    hbm = pl.BlockSpec(memory_space=pltpu.HBM)
    results = pl.pallas_call(
        functools.partial(mixer_kernel, (n_seq, n_head, n_dp, heads, width // heads)),
        out_shape=(
            pltpu.VMEM((tokens, width), b16),
            pltpu.VMEM((tokens, state_size), b16),
            pltpu.VMEM((tokens, state_size), b16),
            pltpu.VMEM((tokens, feats), b16),
            pltpu.VMEM((heads, rows_out), f32),
        ),
        in_specs=[hbm] * 8,
        out_specs=[pl.BlockSpec(memory_space=pltpu.VMEM)] * 5,
        scratch_shapes=[
            pltpu.VMEM((1, heads), f32),
            pltpu.VMEM((1, heads), f32),
            pltpu.VMEM((tokens, feats), b16),
            pltpu.VMEM((2, tokens, width), b16),
            pltpu.VMEM((2, tokens, state_size), b16),
            pltpu.VMEM((tokens, width), b16),
            pltpu.VMEM((tokens, state_size), b16),
            pltpu.VMEM((n_head * heads, feats), b16),
            pltpu.VMEM((n_head * heads, tokens), f32),
            pltpu.VMEM((2 * n_head - 1, heads, tokens), f32),
            pltpu.VMEM((heads, tokens, tokens), f32),
            pltpu.VMEM((heads, tokens, tokens), b16),
            pltpu.VMEM((tokens, tokens), f32),
            pltpu.VMEM((n_head * heads, tokens), b16),
            pltpu.VMEM((n_head * heads, feats), b16),
            pltpu.VMEM((share, heads, rows_out), b16),
            dma((8,)),
            dma((n_head - 1,)),
            dma((n_head - 1,)),
            dma((CHUNKS + 1,)),
            dma((CHUNKS + 1,)),
            dma((2 * n_head - 1,)),
            dma((2 * n_head - 1,)),
            dma((n_head - 1,)),
            dma((n_head - 1,)),
            dma((share,)),
            dma((share,)),
        ],
        compiler_params=pltpu.CompilerParams(
            collective_id=0, has_side_effects=True, vmem_limit_bytes=32 * 1024 * 1024
        ),
        name="mixer",
    )(
        *(
            pltpu.with_memory_space_constraint(a, pltpu.HBM)
            for a in (
                layer_input[0], head_input[0], in_matrix[0], out_matrix[0], grad_output[0],
                jnp.transpose(step_weight), step_bias[None], decay_log[None],
            )
        )
    )
    count = len(results)
    gx, gb, gc, gin, gw = pl.pallas_call(
        write_out,
        out_shape=tuple(jax.ShapeDtypeStruct(a.shape, a.dtype) for a in results),
        in_specs=[pl.BlockSpec(memory_space=pl.ANY)] * count,
        out_specs=[hbm] * count,
        scratch_shapes=[dma((count,))],
        compiler_params=pltpu.CompilerParams(vmem_limit_bytes=4 * 1024 * 1024),
        name="write_out",
    )(*(pltpu.with_memory_space_constraint(a, pltpu.VMEM) for a in results))
    return gx[None], gb[None], gc[None], gin[None], jnp.transpose(gw)


def fits(mesh, args):
    n_seq, n_head, n_dp = (mesh.shape[a] for a in ("seq", "head", "dp"))
    tokens = args[0].shape[1] // n_seq
    return (
        n_seq == 2
        and n_head == G
        and tokens == BLOCK
        and (n_seq * n_dp) % n_head == 0
    )


def solution(mesh):
    in_specs = (
        P("dp", "seq", "head"),
        P("dp", "seq", "head"),
        P("dp", "seq", "head"),
        P("dp", "seq", "head"),
        P("dp", "seq", "head"),
        P(None, "head"),
        P("head"),
        P("head"),
    )
    out_specs = (
        P("dp", "seq", "head"),
        P("dp", "seq", "head"),
        P("dp", "seq", "head"),
        P("dp", "seq", "head"),
        P(("seq", "dp"), "head"),
    )

    def run(*args):
        here = functools.partial(fused_body, mesh) if fits(mesh, args) else body
        return jax.shard_map(
            here, mesh=mesh, in_specs=in_specs, out_specs=out_specs, check_vma=False
        )(*args)

    return run
```

```python
import functools

import jax
import jax.numpy as jnp
from jax import lax
from jax.experimental import pallas as pl
from jax.experimental.pallas import tpu as pltpu
from jax.sharding import PartitionSpec as P

H = 64
P_SIZE = 64
NSTATE = 128
G = 4
BLOCK = 128


PRECISION_LEVEL = lax.Precision.HIGHEST


def prefix(value, axis, join, neutral, backward):
    count = lax.axis_size(axis)
    place = lax.axis_index(axis)
    ahead = count - 1 - place if backward else place
    gathered = jax.tree.map(
        lambda a, kind: lax.all_gather(a.astype(kind), axis), value, (jnp.bfloat16, jnp.bfloat16)
    )
    state = jax.tree.map(lambda a, e: jnp.zeros_like(a) + jnp.asarray(e, a.dtype), value, neutral)

    def one(step, state):
        source = count - 1 - step if backward else step
        return join(
            state,
            jax.tree.map(
                lambda a, own: lax.dynamic_index_in_dim(a, source, 0, False).astype(own.dtype),
                gathered,
                value,
            ),
        )

    return lax.fori_loop(0, ahead, one, state)


def block_step(carry_state, inputs):
    input_block, b_block, c_block, step_block, decay_block = inputs
    cumulated = jnp.cumsum(decay_block, axis=-1)
    block_len = cumulated.shape[-1]
    lower_mask = jnp.arange(block_len)[:, None] >= jnp.arange(block_len)[None, :]
    decay_span = jnp.exp(
        jnp.where(lower_mask, cumulated[..., :, None] - cumulated[..., None, :], -1e30)
    )
    kernel = jnp.einsum("tgn,sgn->gts", c_block, b_block, precision=PRECISION_LEVEL)
    weight_values = kernel[:, None] * decay_span * step_block[..., None, :]
    within_block = jnp.einsum(
        "idwz,zidx->widx", weight_values, input_block, precision=PRECISION_LEVEL
    )
    carried = jnp.einsum("tgn,grnp->tgrp", c_block, carry_state, precision=PRECISION_LEVEL)
    output = within_block + jnp.moveaxis(jnp.exp(cumulated), -1, 0)[..., None] * carried
    totals = cumulated[..., -1]
    inflow = jnp.exp(totals[..., None] - cumulated) * step_block
    fresh_term = jnp.einsum(
        "grs,sgn,sgrp->grnp", inflow, b_block, input_block, precision=PRECISION_LEVEL
    )
    return (jnp.exp(totals)[..., None, None] * carry_state + fresh_term, output)


def segment(x_rows, b_rows, readout_rows, step_sizes, decays, start_state):
    length = x_rows.shape[0]
    blocks = length // BLOCK

    def split_rows(values):
        return values.reshape((blocks, BLOCK) + values.shape[1:])

    def split_last(values):
        return jnp.moveaxis(values.reshape(values.shape[:-1] + (blocks, BLOCK)), -2, 0)

    final_state, outputs = lax.scan(
        block_step,
        start_state,
        (
            split_rows(x_rows),
            split_rows(b_rows),
            split_rows(readout_rows),
            split_last(step_sizes),
            split_last(decays),
        ),
    )
    return (outputs.reshape(x_rows.shape), final_state)


def join_pairs(earlier, later):
    return (earlier[0] + later[0], jnp.exp(later[0])[..., None, None] * earlier[1] + later[1])


def body(
    layer_input, head_input, in_matrix, out_matrix, grad_output, step_weight, step_bias, decay_log
):
    tokens = head_input.shape[1]
    group_count = in_matrix.shape[2] // NSTATE
    ratio = H // G
    heads_here = group_count * ratio
    whole_input = lax.all_gather(layer_input, "head", axis=2, tiled=True)[0]
    preact = jnp.dot(whole_input, step_weight, preferred_element_type=jnp.float32) + step_bias
    step_sizes = jnp.transpose(jax.nn.softplus(preact)).reshape(group_count, ratio, tokens)
    rates = jnp.exp(decay_log).reshape(group_count, ratio)
    decays = -rates[..., None] * step_sizes
    x_rows = head_input[0].astype(jnp.float32).reshape(tokens, group_count, ratio, P_SIZE)
    b_rows = in_matrix[0].astype(jnp.float32).reshape(tokens, group_count, NSTATE)
    readout_rows = out_matrix[0].astype(jnp.float32).reshape(tokens, group_count, NSTATE)
    output_gradient = grad_output[0].astype(jnp.float32).reshape(tokens, group_count, ratio, P_SIZE)
    running_state = jnp.cumsum(decays, axis=-1)
    totals = running_state[..., -1]
    local_state = jnp.einsum(
        "grs,sgn,sgrp->grnp",
        jnp.exp(totals[..., None] - running_state) * step_sizes,
        b_rows,
        x_rows,
        precision=PRECISION_LEVEL,
    )
    local_grad = jnp.einsum(
        "vad,dvm,dvah->vamh",
        jnp.exp(running_state),
        readout_rows,
        output_gradient,
        precision=PRECISION_LEVEL,
    )
    neutral = (jnp.zeros_like(totals), jnp.zeros_like(local_state))
    incoming = prefix((totals, local_state), "seq", join_pairs, neutral, False)[1]
    outgoing = prefix((totals, local_grad), "seq", join_pairs, neutral, True)[1]

    def local_map(x_arg, b_arg, c_arg, step_arg):
        return segment(x_arg, b_arg, c_arg, step_arg, -rates[..., None] * step_arg, incoming)

    forward_out, pullback = jax.vjp(local_map, x_rows, b_rows, readout_rows, step_sizes)
    grad_x, grad_b, grad_c, grad_step = pullback((output_gradient, outgoing))
    grad_pre = (
        jnp.transpose(grad_step.reshape(heads_here, tokens)) * jax.nn.sigmoid(preact)
    ).astype(jnp.bfloat16)
    partial_terms = lax.dot_general(
        grad_pre, step_weight, (((1,), (1,)), ((), ())), preferred_element_type=jnp.float32
    )
    grad_input = lax.psum_scatter(
        partial_terms.astype(jnp.bfloat16), "head", scatter_dimension=1, tiled=True
    )
    seq_part = lax.psum_scatter(
        lax.dot_general(
            whole_input, grad_pre, (((0,), (0,)), ((), ())), preferred_element_type=jnp.float32
        ).astype(jnp.bfloat16),
        "seq",
        scatter_dimension=0,
        tiled=True,
    ).astype(jnp.float32)
    grad_weight = lax.psum_scatter(seq_part, "dp", scatter_dimension=0, tiled=True)
    return (
        grad_x.reshape(tokens, heads_here * P_SIZE).astype(jnp.bfloat16)[None],
        grad_b.reshape(tokens, group_count * NSTATE).astype(jnp.bfloat16)[None],
        grad_c.reshape(tokens, group_count * NSTATE).astype(jnp.bfloat16)[None],
        grad_input[None],
        grad_weight,
    )


MESH = pl.DeviceIdType.MESH
CHUNKS = 4
NT = (((1,), (1,)), ((), ()))
NN = (((1,), (0,)), ((), ()))
TN = (((0,), (0,)), ((), ()))


def mm(a, b, dims):
    return lax.dot_general(a, b, dims, preferred_element_type=jnp.float32)


def exact_mm(a, ones):
    count = a.shape[0]
    parts = []
    for _ in range(3):
        parts.append(a.astype(jnp.bfloat16))
        a = a - parts[-1].astype(jnp.float32)
    sums = mm(jnp.concatenate(parts, axis=0), ones, NN)
    return sums[:count] + (sums[count : 2 * count] + sums[2 * count :])


def two_parts(v):
    high = v.astype(jnp.bfloat16)
    low = (v - high.astype(jnp.float32)).astype(jnp.bfloat16)
    return high, low


def softplus(v):
    return jnp.maximum(v, 0.0) + jnp.log1p(jnp.exp(-jnp.abs(v)))


def mixer_kernel(
    sizes,
    layer_hbm, x_hbm, b_hbm, c_hbm, gy_hbm, w_hbm, bias_hbm, rate_hbm,
    gx_ref, gb_ref, gc_ref, gin_ref, gw_ref,
    bias_ref, rate_ref, layer, xg, bc, far_xg, far_bc, w_all, part, part_far, mt, ke, qcol, gp_all, gw_send, gw_recv,
    load_sem, w_send, w_recv, raw_send, raw_recv, p_send, p_recv, g_send, g_recv, d_send, d_recv,
):
    n_seq, n_head, n_dp, heads, p_size = sizes
    tokens, feats = layer.shape
    me_s, me_h, me_d = lax.axis_index("seq"), lax.axis_index("head"), lax.axis_index("dp")
    far_s = 1 - me_s
    rows_out = gw_ref.shape[1]
    cuts = feats // rows_out
    share = n_seq * n_dp

    def head_at(k):
        return lax.rem(me_h + k, n_head)

    def place(s, h, d):
        return {"seq": s, "head": h, "dp": d}

    loads = [
        pltpu.make_async_copy(x_hbm, xg.at[0], load_sem.at[0]),
        pltpu.make_async_copy(gy_hbm, xg.at[1], load_sem.at[1]),
        pltpu.make_async_copy(b_hbm, bc.at[0], load_sem.at[2]),
        pltpu.make_async_copy(c_hbm, bc.at[1], load_sem.at[3]),
        pltpu.make_async_copy(layer_hbm, layer, load_sem.at[4]),
        pltpu.make_async_copy(
            w_hbm.at[:, pl.ds(pl.multiple_of(me_h * feats, feats), feats)],
            w_all.at[pl.ds(pl.multiple_of(me_h * heads, heads), heads)],
            load_sem.at[5],
        ),
        pltpu.make_async_copy(bias_hbm, bias_ref, load_sem.at[6]),
        pltpu.make_async_copy(rate_hbm, rate_ref, load_sem.at[7]),
    ]

    barrier = pltpu.get_barrier_semaphore()
    my_row = me_s * n_dp + me_d
    source_h = my_row // cuts
    for k in range(n_head):
        if k:
            pl.semaphore_signal(
                barrier, inc=1, device_id=place(me_s, head_at(k), me_d), device_id_type=MESH
            )
        pl.semaphore_signal(
            barrier, inc=1, device_id=place(far_s, head_at(k), me_d), device_id_type=MESH
        )
    mine = source_h == me_h
    for k in range(share):
        spot = lax.rem(my_row + k, share)

        def greet():
            pl.semaphore_signal(
                barrier,
                inc=1,
                device_id=place(spot // n_dp, source_h, lax.rem(spot, n_dp)),
                device_id_type=MESH,
            )

        if k:
            greet()
        else:
            pl.when(jnp.logical_not(mine))(greet)
    for load in loads:
        load.start()
    pl.semaphore_wait(barrier, 2 * n_head - 1 + share - jnp.where(mine, 1, 0))

    w_copies = []
    for k in range(1, n_head):
        to = head_at(k)
        copy = pltpu.make_async_remote_copy(
            src_ref=w_hbm.at[:, pl.ds(pl.multiple_of(to * feats, feats), feats)],
            dst_ref=w_all.at[pl.ds(pl.multiple_of(me_h * heads, heads), heads)],
            send_sem=w_send.at[k - 1],
            recv_sem=w_recv.at[k - 1],
            device_id=place(me_s, to, me_d),
            device_id_type=MESH,
        )
        copy.start()
        w_copies.append(copy)

    for load in loads[:4]:
        load.wait()
    raw_copies = []
    width = far_xg.shape[1] // CHUNKS
    chunks = [slice(c * width, (c + 1) * width) for c in range(CHUNKS)]
    near_refs = [bc.at[me_s]] + [xg.at[me_s, :, lanes] for lanes in chunks]
    far_refs = [far_bc] + [far_xg.at[:, lanes] for lanes in chunks]
    for at in range(CHUNKS + 1):
        copy = pltpu.make_async_remote_copy(
            src_ref=near_refs[at],
            dst_ref=far_refs[at],
            send_sem=raw_send.at[at],
            recv_sem=raw_recv.at[at],
            device_id=place(far_s, me_h, me_d),
            device_id_type=MESH,
        )
        raw_copies.append(copy)
    for copy in raw_copies[:CHUNKS]:
        copy.start()

    pair = 2 * p_size
    left = lax.broadcasted_iota(jnp.int32, (tokens, pair), 1) < p_size
    kt = mm(bc[0], bc[1], NT)
    zero_pair = jnp.zeros((tokens, pair), jnp.bfloat16)
    for j in range(heads // 2):
        lanes = slice(j * pair, (j + 1) * pair)
        x_pair, gy_pair = xg[0, :, lanes], xg[1, :, lanes]
        mt[2 * j] = mm(jnp.where(left, x_pair, zero_pair), gy_pair, NT)
        mt[2 * j + 1] = mm(jnp.where(left, zero_pair, x_pair), gy_pair, NT)

    upper = (
        lax.broadcasted_iota(jnp.int32, (tokens, tokens), 0)
        <= lax.broadcasted_iota(jnp.int32, (tokens, tokens), 1)
    )
    summing = jnp.where(upper, 1.0, 0.0).astype(jnp.bfloat16)
    lower = jnp.where(
        lax.broadcasted_iota(jnp.int32, (tokens, tokens), 0)
        >= lax.broadcasted_iota(jnp.int32, (tokens, tokens), 1),
        1.0,
        0.0,
    ).astype(jnp.bfloat16)
    square = lax.broadcasted_iota(jnp.int32, (heads, heads), 0) == lax.broadcasted_iota(
        jnp.int32, (heads, heads), 1
    )

    def column(row):
        return jnp.sum(jnp.where(square, row, 0.0), axis=1, keepdims=True)

    spread_rows = lax.rem(lax.broadcasted_iota(jnp.int32, (2 * heads, heads * p_size), 0), heads)
    spread_at = lax.broadcasted_iota(jnp.int32, (2 * heads, heads * p_size), 1) // p_size
    spread = jnp.where(spread_rows == spread_at, 1.0, 0.0).astype(jnp.bfloat16)

    def widen(v):
        high, low = two_parts(v)
        return mm(jnp.concatenate([high, low], axis=0), spread, TN)

    for load in loads[4:]:
        load.wait()
    bias = column(bias_ref[...])
    rate = jnp.exp(column(rate_ref[...]))
    for copy in w_copies:
        copy.wait_recv()
    part[...] = mm(w_all[...], layer[...], NT)
    part_copies = {}
    for hop in range(2):
        for k in range(1 - hop, n_head):
            to = head_at(k)
            at = 2 * k + hop - 1
            copy = pltpu.make_async_remote_copy(
                src_ref=part.at[pl.ds(pl.multiple_of(to * heads, heads), heads)],
                dst_ref=part_far.at[at],
                send_sem=p_send.at[at],
                recv_sem=p_recv.at[at],
                device_id=place(far_s if hop else me_s, to, me_d),
                device_id_type=MESH,
            )
            copy.start()
            part_copies[at] = copy
    for copy in raw_copies[CHUNKS:]:
        copy.start()

    for k in range(1, n_head):
        part_copies[2 * k - 1].wait_recv()
    preact = part[pl.ds(pl.multiple_of(me_h * heads, heads), heads), :] + bias
    for k in range(1, n_head):
        preact = preact + part_far[2 * k - 1]
    dt = softplus(preact)
    cum = exact_mm(-rate * dt, summing)
    total = cum[:, tokens - 1 :]
    cum_col = jnp.transpose(cum)
    dt_col = jnp.transpose(dt)
    dkt = jnp.zeros((tokens, tokens), jnp.float32)
    r_rows = []
    for h in range(heads):
        if h == heads // 2:
            first = me_s == 0
            for k in range(n_head):
                part_copies[2 * k].wait_recv()
            far_pre = bias
            for k in range(n_head):
                far_pre = far_pre + part_far[2 * k]
            far_dt = softplus(far_pre)
            far_cum = exact_mm(-rate * far_dt, summing)
            far_total = far_cum[:, tokens - 1 :]
            from_start = jnp.exp(cum)
            to_end = jnp.exp(total - cum)
            far_scale = jnp.where(first, jnp.exp(far_cum), jnp.exp(far_total - far_cum) * far_dt)
            near_scale = jnp.where(first, to_end * dt, from_start)
            far_wide = widen(far_scale)
            near_wide = widen(near_scale)
        gap = cum[h : h + 1, :] - cum_col[:, h : h + 1]
        span = jnp.exp(jnp.where(upper, gap, -1e30))
        ke[h] = (kt * span).astype(jnp.bfloat16)
        step_here = dt_col[:, h : h + 1]
        f = mt[h] * span
        dkt = dkt + f * step_here
        prod = f * kt
        qcol[:, h : h + 1] = jnp.sum(prod, axis=1, keepdims=True)
        r_rows.append(jnp.sum(prod * step_here, axis=0, keepdims=True))
    r = jnp.concatenate(r_rows, axis=0)
    q = jnp.transpose(qcol[...])[:heads]

    raw_copies[0].wait_recv()
    far_rows = far_bc[...]
    near_rows = bc[me_s]
    states, carried, inputs = [], [], []
    w = jnp.zeros((heads, tokens), jnp.float32)
    for c, lanes in enumerate(chunks):
        if c % (CHUNKS // 2) == 0:
            for copy in raw_copies[1 + c : 1 + c + CHUNKS // 2]:
                copy.wait_recv()
        scaled = far_xg[:, lanes].astype(jnp.float32) * far_wide[:, lanes]
        states.append(mm(far_rows, scaled.astype(jnp.bfloat16), TN).astype(jnp.bfloat16))
        carried.append(mm(near_rows, states[c], NN))
        inputs.append(xg[me_s, :, lanes].astype(jnp.float32))
        high, low = two_parts(inputs[c] * carried[c])
        w = w + mm(spread[:heads, lanes], high, NT) + mm(spread[:heads, lanes], low, NT)

    v = to_end * w
    q = jnp.where(first, q + v, q)
    da = r - dt * q + jnp.where(first, 0.0, from_start * w)
    at_end = jnp.where(first, jnp.sum(dt * v, axis=1, keepdims=True), 0.0)
    grad_step = q - rate * (exact_mm(da, lower) + at_end)
    my_rows = pl.ds(pl.multiple_of(me_h * heads, heads), heads)
    gp_all[my_rows, :] = (grad_step * jax.nn.sigmoid(preact)).astype(jnp.bfloat16)
    gp_copies = []
    for k in range(1, n_head):
        copy = pltpu.make_async_remote_copy(
            src_ref=gp_all.at[my_rows],
            dst_ref=gp_all.at[my_rows],
            send_sem=g_send.at[k - 1],
            recv_sem=g_recv.at[k - 1],
            device_id=place(me_s, head_at(k), me_d),
            device_id_type=MESH,
        )
        copy.start()
        gp_copies.append(copy)

    dt_wide = widen(dt)
    flag = jnp.where(first, 1.0, 0.0)
    brought = jnp.concatenate(carried, axis=1)
    for j in range(heads // 2):
        lanes = slice(j * pair, (j + 1) * pair)
        gy_pair = xg[1, :, lanes]
        inner = jnp.where(left, mm(ke[2 * j], gy_pair, NN), mm(ke[2 * j + 1], gy_pair, NN))
        gx_ref[:, lanes] = (
            inner * dt_wide[:, lanes] + flag * near_wide[:, lanes] * brought[:, lanes]
        ).astype(jnp.bfloat16)

    for copy in gp_copies:
        copy.wait_recv()
    gw_send[...] = mm(gp_all[...], layer[...], NN).astype(jnp.bfloat16)
    gw_copies = []
    for cut in range(cuts):
        row = me_h * cuts + cut
        to_s, to_d = row // n_dp, lax.rem(row, n_dp)
        for k in range(n_head):
            to = head_at(k)
            at = cut * n_head + k
            block = gw_send.at[
                pl.ds(pl.multiple_of(to * heads, heads), heads),
                cut * rows_out : (cut + 1) * rows_out,
            ]
            copy = pltpu.make_async_remote_copy(
                src_ref=block,
                dst_ref=gw_recv.at[my_row],
                send_sem=d_send.at[at],
                recv_sem=d_recv.at[my_row],
                device_id=place(to_s, to, to_d),
                device_id_type=MESH,
            )
            if k:
                copy.start()
                gw_copies.append((copy, None))
            else:
                away = row != my_row
                pl.when(away)(copy.start)
                gw_copies.append((copy, away))

                @pl.when(jnp.logical_not(away))
                def _():
                    gw_recv[my_row] = block[...]

    extra = jnp.zeros_like(dkt)
    for c, lanes in enumerate(chunks):
        extra = extra + mm((inputs[c] * near_wide[:, lanes]).astype(jnp.bfloat16), states[c], NT)
    dk = dkt.astype(jnp.bfloat16)
    gb_ref[...] = (mm(dk, bc[1], NN) + flag * extra).astype(jnp.bfloat16)
    gc_ref[...] = (mm(dk, bc[0], TN) + (1.0 - flag) * extra).astype(jnp.bfloat16)

    gin = jnp.zeros((tokens, feats), jnp.float32)
    for j in range(n_head):
        rows = slice(j * heads, (j + 1) * heads)
        term = mm(gp_all[rows, :], w_all[rows, :], TN)
        gin = gin + term.astype(jnp.bfloat16).astype(jnp.float32)
    gin_ref[...] = gin.astype(jnp.bfloat16)

    def arrived(k):
        spot = lax.rem(my_row + k, share)
        return pltpu.make_async_remote_copy(
            src_ref=gw_recv.at[spot],
            dst_ref=gw_recv.at[spot],
            send_sem=d_send.at[0],
            recv_sem=d_recv.at[spot],
            device_id=place(far_s, me_h, me_d),
            device_id_type=MESH,
        )

    for k in range(1, share):
        arrived(k).wait_recv()
    pl.when(jnp.logical_not(mine))(arrived(0).wait_recv)
    gw = gw_recv[0].astype(jnp.float32)
    for k in range(1, share):
        gw = gw + gw_recv[k].astype(jnp.float32)
    gw_ref[...] = gw

    for copy in w_copies + raw_copies + list(part_copies.values()) + gp_copies:
        copy.wait_send()
    for copy, away in gw_copies:
        if away is None:
            copy.wait_send()
        else:
            pl.when(away)(copy.wait_send)


def write_out(*refs):
    sems = refs[-1]
    count = len(refs) // 2
    copies = [
        pltpu.make_async_copy(refs[i], refs[count + i], sems.at[i]) for i in range(count)
    ]
    for copy in copies:
        copy.start()
    for copy in copies:
        copy.wait()


def fused_body(
    mesh, layer_input, head_input, in_matrix, out_matrix, grad_output, step_weight, step_bias, decay_log
):
    n_seq, n_head, n_dp = (mesh.shape[a] for a in ("seq", "head", "dp"))
    tokens, feats = layer_input.shape[1:]
    width = head_input.shape[2]
    state_size = in_matrix.shape[2]
    heads = step_bias.shape[0]
    rows_out = step_weight.shape[0] // (n_seq * n_dp)
    share = n_seq * n_dp
    b16, f32 = jnp.bfloat16, jnp.float32
    dma = pltpu.SemaphoreType.DMA
    hbm = pl.BlockSpec(memory_space=pltpu.HBM)
    results = pl.pallas_call(
        functools.partial(mixer_kernel, (n_seq, n_head, n_dp, heads, width // heads)),
        out_shape=(
            pltpu.VMEM((tokens, width), b16),
            pltpu.VMEM((tokens, state_size), b16),
            pltpu.VMEM((tokens, state_size), b16),
            pltpu.VMEM((tokens, feats), b16),
            pltpu.VMEM((heads, rows_out), f32),
        ),
        in_specs=[hbm] * 8,
        out_specs=[pl.BlockSpec(memory_space=pltpu.VMEM)] * 5,
        scratch_shapes=[
            pltpu.VMEM((1, heads), f32),
            pltpu.VMEM((1, heads), f32),
            pltpu.VMEM((tokens, feats), b16),
            pltpu.VMEM((2, tokens, width), b16),
            pltpu.VMEM((2, tokens, state_size), b16),
            pltpu.VMEM((tokens, width), b16),
            pltpu.VMEM((tokens, state_size), b16),
            pltpu.VMEM((n_head * heads, feats), b16),
            pltpu.VMEM((n_head * heads, tokens), f32),
            pltpu.VMEM((2 * n_head - 1, heads, tokens), f32),
            pltpu.VMEM((heads, tokens, tokens), f32),
            pltpu.VMEM((heads, tokens, tokens), b16),
            pltpu.VMEM((tokens, tokens), f32),
            pltpu.VMEM((n_head * heads, tokens), b16),
            pltpu.VMEM((n_head * heads, feats), b16),
            pltpu.VMEM((share, heads, rows_out), b16),
            dma((8,)),
            dma((n_head - 1,)),
            dma((n_head - 1,)),
            dma((CHUNKS + 1,)),
            dma((CHUNKS + 1,)),
            dma((2 * n_head - 1,)),
            dma((2 * n_head - 1,)),
            dma((n_head - 1,)),
            dma((n_head - 1,)),
            dma((share,)),
            dma((share,)),
        ],
        compiler_params=pltpu.CompilerParams(
            collective_id=0, has_side_effects=True, vmem_limit_bytes=32 * 1024 * 1024
        ),
        name="mixer",
    )(
        *(
            pltpu.with_memory_space_constraint(a, pltpu.HBM)
            for a in (
                layer_input[0], head_input[0], in_matrix[0], out_matrix[0], grad_output[0],
                jnp.transpose(step_weight), step_bias[None], decay_log[None],
            )
        )
    )
    count = len(results)
    gx, gb, gc, gin, gw = pl.pallas_call(
        write_out,
        out_shape=tuple(jax.ShapeDtypeStruct(a.shape, a.dtype) for a in results),
        in_specs=[pl.BlockSpec(memory_space=pl.ANY)] * count,
        out_specs=[hbm] * count,
        scratch_shapes=[dma((count,))],
        compiler_params=pltpu.CompilerParams(vmem_limit_bytes=4 * 1024 * 1024),
        name="write_out",
    )(*(pltpu.with_memory_space_constraint(a, pltpu.VMEM) for a in results))
    return gx[None], gb[None], gc[None], gin[None], jnp.transpose(gw)


def fits(mesh, args):
    n_seq, n_head, n_dp = (mesh.shape[a] for a in ("seq", "head", "dp"))
    tokens = args[0].shape[1] // n_seq
    return (
        n_seq == 2
        and n_head == G
        and tokens == BLOCK
        and (n_seq * n_dp) % n_head == 0
    )


def solution(mesh):
    in_specs = (
        P("dp", "seq", "head"),
        P("dp", "seq", "head"),
        P("dp", "seq", "head"),
        P("dp", "seq", "head"),
        P("dp", "seq", "head"),
        P(None, "head"),
        P("head"),
        P("head"),
    )
    out_specs = (
        P("dp", "seq", "head"),
        P("dp", "seq", "head"),
        P("dp", "seq", "head"),
        P("dp", "seq", "head"),
        P(("seq", "dp"), "head"),
    )

    def run(*args):
        here = functools.partial(fused_body, mesh) if fits(mesh, args) else body
        return jax.shard_map(
            here, mesh=mesh, in_specs=in_specs, out_specs=out_specs, check_vma=False
        )(*args)

    return run
```
